256 devices in a mesh: section: 2 (over x_lo), dp: 8 (over y, core), tensor: 16 (over z, x_hi).
Axes of the slice: x: 4 (x_hi: 2, x_lo: 2; x = x_hi * 2 + x_lo), y: 4, z: 8, core: 2. Of those that a mesh axis runs over, the one named last changes fastest.
Arguments:
- segment_input: bfloat16 [2, 2048, 12288], P('section', ('dp', 'tensor')), may hold values from -6 to 6
- context: bfloat16 [2, 2048, 6144], P('section', 'dp', 'tensor'), may hold values from -8 to 8
- out_proj: bfloat16 [2, 12288, 6144], P('section', None, 'tensor'), may hold values from -0.078125 to 0.078125
- grad_output: bfloat16 [2, 2048, 12288], P('section', ('dp', 'tensor')), may hold values from -24 to 24
Outputs:
- forward: bfloat16 [2, 2048, 12288], P('section', ('dp', 'tensor'))
- moved: bfloat16 [2, 2048, 12288], P('section', ('dp', 'tensor'))
- context_grad: bfloat16 [2, 2048, 6144], P('section', 'dp', 'tensor')
- proj_grad: bfloat16 [2, 12288, 6144], P('section', 'dp', 'tensor')
The draws below stay inside these ranges and needn't reach their ends.
All inputs are finite; a program needn't handle non-finite values.
Results may differ from the reference program's by a relative error of at most 0.02.
Values may be sent and summed in bfloat16 or wider, within the bound.
No kernel may reach another device: no remote copies, remote signals or barrier semaphores. Data moves between devices by JAX's collectives and lax.ppermute only.
A program may use at most 128 MiB of HBM per device.

```python
import math
import jax
import jax.numpy as jnp
from jax import lax

D = 12288
TOK_DEV = 256
HK = 6144
TOKENS = 2048
N_SECTION = 2
N_DP = 8
N_TENSOR = 16


def spiked(values, stream_key, source, target, shards_of, factor):
    def block_of(dim):
        return (jnp.arange(values.shape[dim]) // (values.shape[dim] // shards_of)).reshape((-1,) + (1,) * (values.ndim - 1 - dim))

    near = jax.random.permutation(stream_key, shards_of)[block_of(target)]
    second = (block_of(target) + shards_of // 2) % shards_of
    return jnp.where((block_of(source) == near) | (block_of(source) == second), factor * values, values)


def shard_levels(stream_key, shape, pieces, smallest, high):
    gain = 1.0
    for axis_at, shards_of in pieces:
        draws = jax.random.uniform(jax.random.fold_in(jax.random.fold_in(stream_key, 6), axis_at), (shards_of,), jnp.float32, smallest / len(pieces), high / len(pieces))
        gain = gain * jnp.repeat(jnp.exp(draws), shape[axis_at] // shards_of).reshape((-1,) + (1,) * (len(shape) - 1 - axis_at))
    return gain


def scatter_about(stream_key, shape, scale, limit, split=(), held_as=jnp.bfloat16):
    factor_of = shard_levels(stream_key, shape, split, -0.22, 0.18) if split else 1.0
    result = jax.random.normal(stream_key, shape, jnp.float32) * scale * factor_of
    return jnp.minimum(jnp.maximum(result, -limit), limit).astype(held_as)


def gaussian_with(rng, shape, scale, most, pieces, heavy, kind=jnp.bfloat16):
    array = scale * jax.random.normal(rng, shape, jnp.float32)
    if pieces:
        array = array * shard_levels(rng, shape, pieces, -0.22, 0.18)
    return jnp.clip(spiked(array, jax.random.fold_in(rng, 3), *heavy), -most, most).astype(kind)


def setup_inputs(seed: int = 0) -> dict:
    seeds = jax.random.split(jax.random.key(seed), 5)
    return {
        "segment_input": scatter_about(seeds[0], (N_SECTION, TOKENS, D), 1.0, 6.0, ((0, 2), (1, 128))),
        "context": gaussian_with(seeds[1], (N_SECTION, TOKENS, HK), 1.0, 8.0, ((0, 2), (1, 8), (2, 16)), (2, 1, 16, 2.0)),
        "out_proj": scatter_about(seeds[2], (N_SECTION, D, HK), HK ** -0.5, 0.078125, ((0, 2), (2, 16))),
        "grad_output": gaussian_with(seeds[3], (N_SECTION, TOKENS, D), 1.0, 24.0, ((0, 2), (1, 128)), (1, 2, 128, 5.5)),
    }


def branch_sum(contexts, weights):
    width = HK // N_TENSOR

    def add_block(carry, block_index):
        ctx_block = lax.dynamic_slice_in_dim(contexts, block_index * width, width, 1)
        weight_block = lax.dynamic_slice_in_dim(weights, block_index * width, width, 1)
        partial_term = lax.dot_general(ctx_block, weight_block, (((1,), (1,)), ((), ())), preferred_element_type=jnp.float32)
        rounded = lax.optimization_barrier(partial_term.astype(jnp.bfloat16))
        return (carry + rounded.astype(jnp.float32), None)
    start_sum = jnp.zeros((TOKENS, D), jnp.float32)
    summed, unused = lax.scan(add_block, start_sum, jnp.arange(N_TENSOR, dtype=jnp.int32))
    return summed

def weight_gradient(upstream, contexts):
    norm_factor = 1.0 / math.sqrt(TOKENS)

    def add_group(carry, group_index):
        grad_block = lax.dynamic_slice_in_dim(upstream, group_index * TOK_DEV, TOK_DEV, 0)
        ctx_block = lax.dynamic_slice_in_dim(contexts, group_index * TOK_DEV, TOK_DEV, 0)
        partial_term = lax.dot_general(grad_block, ctx_block, (((0,), (0,)), ((), ())), preferred_element_type=jnp.float32)
        rounded = lax.optimization_barrier((norm_factor * partial_term).astype(jnp.bfloat16))
        return (carry + rounded.astype(jnp.float32), None)
    start_sum = jnp.zeros((D, HK), jnp.float32)
    summed, unused = lax.scan(add_group, start_sum, jnp.arange(N_DP, dtype=jnp.int32))
    return summed.astype(jnp.bfloat16)

def reference(segment_input, context, out_proj, grad_output):
    outputs = []
    ctx_grads = []
    proj_grads = []
    for section in range(2):
        branch = branch_sum(context[section], out_proj[section])
        outputs.append((segment_input[section].astype(jnp.float32) + branch).astype(jnp.bfloat16))
        ctx_grads.append(jnp.dot(grad_output[section], out_proj[section], preferred_element_type=jnp.float32).astype(jnp.bfloat16))
        proj_grads.append(weight_gradient(grad_output[section], context[section]))
    forward = jnp.stack(outputs)
    moved = jnp.stack([grad_output[1], forward[0]])
    return (forward, moved, jnp.stack(ctx_grads), jnp.stack(proj_grads))
```

```python
import math

import jax
import jax.numpy as jnp
from jax import lax
from jax.sharding import Mesh
from jax.sharding import PartitionSpec as P

BF16 = jnp.bfloat16
F32 = jnp.float32
GROUP = ("y", "core", "xh")


def shift(value, axis, by):
    n = lax.axis_size(axis)
    return lax.ppermute(value, axis, [(i, (i + by) % n) for i in range(n)])


def swap(value, axis):
    return shift(value, axis, 1)


def add(a, b):
    return (a.astype(F32) + b.astype(F32)).astype(BF16)


def wrap(index, n):
    return index & (n - 1)


def pick(stack, index):
    return lax.dynamic_index_in_dim(stack, index, 0, keepdims=False)


def place(buffer, block, starts):
    return lax.dynamic_update_slice(buffer, block, starts)


def ring_sum(chunk_of, position, axis):
    n = lax.axis_size(axis)
    far = n // 2
    opposite = chunk_of(wrap(position + far, n))
    half = opposite.shape[-1] // 2
    right = shift(opposite[..., :half], axis, 1)
    left = shift(opposite[..., half:], axis, -1)
    for away in range(far - 1, 0, -1):
        ahead = chunk_of(wrap(position + away, n))
        behind = chunk_of(wrap(position - away, n))
        if away == far - 1:
            right = jnp.concatenate([add(ahead[..., :half], right), ahead[..., half:]], -1)
            left = jnp.concatenate([behind[..., :half], add(behind[..., half:], left)], -1)
        else:
            right = add(ahead, right)
            left = add(behind, left)
        right = shift(right, axis, 1)
        left = shift(left, axis, -1)
    own = chunk_of(position)
    return (own.astype(F32) + right.astype(F32) + left.astype(F32)).astype(BF16)


def ring_gather(block, axis):
    n = lax.axis_size(axis)
    far = n // 2
    half = block.shape[0] // 2
    blocks = {0: block}
    right = left = block
    for away in range(1, far):
        right = shift(right, axis, 1)
        left = shift(left, axis, -1)
        blocks[-away] = right
        blocks[away] = left
    blocks[far] = jnp.concatenate([shift(right[:half], axis, 1), shift(left[half:], axis, -1)], 0)
    return blocks


def shards(segment_input, context, out_proj, grad_output):
    residual = segment_input[0]
    contexts = context[0]
    weights = out_proj[0]
    upstream = grad_output[0]
    y, core, z, xh = (lax.axis_index(name) for name in ("y", "core", "z", "xh"))
    n_y, n_core, n_z, n_xh = (lax.axis_size(name) for name in ("y", "core", "z", "xh"))
    n_group = n_y * n_core * n_xh
    own_count, model = upstream.shape
    group_tokens, width = contexts.shape
    features = model // n_group
    tokens = group_tokens * n_y * n_core
    z_tokens = own_count * n_xh

    both = jnp.concatenate([contexts, swap(contexts, "xh")], 1)
    row = (y * n_core + core) * n_xh
    own_rows = lax.dynamic_slice_in_dim(weights, (row + xh) * features, features, 0)
    partner_rows = lax.dynamic_slice_in_dim(weights, (row + 1 - xh) * features, features, 0)
    block = jnp.concatenate([own_rows, swap(partner_rows, "xh")], 1)

    spread = upstream.reshape(own_count, n_group, features).transpose(1, 0, 2)
    spread = lax.all_to_all(spread, GROUP, 0, 0, tiled=True)
    grad_blocks = ring_gather(spread.reshape(n_group * own_count, features), "z")

    ctx_all = jnp.zeros((n_z, n_y, n_core, z_tokens, 2 * width), BF16)
    for away, piece in ring_gather(both, "y").items():
        there = wrap(y + away, n_y)
        for at, part in ((core, piece), (1 - core, swap(piece, "core"))):
            ctx_all = place(ctx_all, part.reshape(n_z, 1, 1, z_tokens, 2 * width), (0, there, at, 0, 0))
    ctx_flat = ctx_all.reshape(tokens, 2 * width)

    partial_branch = lax.dot_general(
        ctx_flat, block, (((1,), (1,)), ((), ())), preferred_element_type=F32
    ).astype(BF16).reshape(n_z, tokens // n_z, features)
    branch = ring_sum(lambda at: pick(partial_branch, at), z, "z")
    branch = lax.all_to_all(branch.reshape(n_group, own_count, features), GROUP, 0, 0, tiled=True)
    branch = branch.transpose(1, 0, 2).reshape(own_count, model)
    forward = add(residual, branch)
    outgoing = jnp.where(lax.axis_index("section") == 0, forward, upstream)
    received = swap(outgoing, "section")

    grad_all = jnp.zeros((n_z, tokens // n_z, features), BF16)
    for away, piece in grad_blocks.items():
        grad_all = place(grad_all, piece[None], (wrap(z + away, n_z), 0, 0))
    grad_flat = grad_all.reshape(tokens, features)

    partial_ctx = jnp.dot(grad_flat, block, preferred_element_type=F32).astype(BF16)
    partial_ctx = partial_ctx.reshape(n_z, n_y, n_core, z_tokens, 2 * width)
    other = lax.dynamic_index_in_dim(partial_ctx, 1 - core, 2, keepdims=False)
    mine = lax.dynamic_index_in_dim(partial_ctx, core, 2, keepdims=False)
    by_y = add(mine, swap(other, "core"))
    summed = ring_sum(lambda at: lax.dynamic_index_in_dim(by_y, at, 1, keepdims=False), y, "y")
    summed = summed.reshape(group_tokens, 2 * width)
    ctx_grad = add(summed[:, :width], swap(summed[:, width:], "xh"))

    norm_factor = 1.0 / math.sqrt(tokens)
    product = lax.dot_general(grad_flat, ctx_flat, (((0,), (0,)), ((), ())), preferred_element_type=F32)
    product = (norm_factor * product).astype(BF16)
    kept = product[:, :width]
    came = swap(product[:, width:], "xh")
    first = xh == 0
    weight_grad = jnp.concatenate([jnp.where(first, kept, came), jnp.where(first, came, kept)], 0)
    return (forward[None], received[None], ctx_grad[None], weight_grad[None])


def solution(mesh):
    fine = Mesh(mesh.devices.reshape(2, 4, 2, 8, 2), ("section", "y", "core", "z", "xh"))
    tokens = P("section", ("y", "core", "z", "xh"), None)
    heads = P("section", ("y", "core"), ("z", "xh"))
    return jax.shard_map(
        shards,
        mesh=fine,
        in_specs=(tokens, heads, P("section", None, ("z", "xh")), tokens),
        out_specs=(tokens, tokens, heads, heads),
        check_vma=False,
    )
```

```python
import math

import jax
import jax.numpy as jnp
from jax import lax
from jax.sharding import Mesh
from jax.sharding import PartitionSpec as P

BF16 = jnp.bfloat16
F32 = jnp.float32
GROUP = ("y", "core", "xh")


def shift(value, axis, by):
    n = lax.axis_size(axis)
    return lax.ppermute(value, axis, [(i, (i + by) % n) for i in range(n)])


def swap(value, axis):
    return shift(value, axis, 1)


def add(a, b):
    return (a.astype(F32) + b.astype(F32)).astype(BF16)


def wrap(index, n):
    return index & (n - 1)


def pick(stack, index):
    return lax.dynamic_index_in_dim(stack, index, 0, keepdims=False)


def place(buffer, block, starts):
    return lax.dynamic_update_slice(buffer, block, starts)


def ring_sum(chunk_of, position, axis):
    n = lax.axis_size(axis)
    far = n // 2
    opposite = chunk_of(wrap(position + far, n))
    half = opposite.shape[-1] // 2
    right = shift(opposite[..., :half], axis, 1)
    left = shift(opposite[..., half:], axis, -1)
    for away in range(far - 1, 0, -1):
        ahead = chunk_of(wrap(position + away, n))
        behind = chunk_of(wrap(position - away, n))
        if away == far - 1:
            right = jnp.concatenate([add(ahead[..., :half], right), ahead[..., half:]], -1)
            left = jnp.concatenate([behind[..., :half], add(behind[..., half:], left)], -1)
        else:
            right = add(ahead, right)
            left = add(behind, left)
        right = shift(right, axis, 1)
        left = shift(left, axis, -1)
    own = chunk_of(position)
    return (own.astype(F32) + right.astype(F32) + left.astype(F32)).astype(BF16)


def ring_gather(block, axis):
    n = lax.axis_size(axis)
    far = n // 2
    half = block.shape[0] // 2
    blocks = {0: block}
    right = left = block
    for away in range(1, far):
        right = shift(right, axis, 1)
        left = shift(left, axis, -1)
        blocks[-away] = right
        blocks[away] = left
    blocks[far] = jnp.concatenate([shift(right[:half], axis, 1), shift(left[half:], axis, -1)], 0)
    return blocks


def shards(segment_input, context, out_proj, grad_output):
    residual = segment_input[0]
    contexts = context[0]
    weights = out_proj[0]
    upstream = grad_output[0]
    y, core, z, xh = (lax.axis_index(name) for name in ("y", "core", "z", "xh"))
    n_y, n_core, n_z, n_xh = (lax.axis_size(name) for name in ("y", "core", "z", "xh"))
    n_group = n_y * n_core * n_xh
    own_count, model = upstream.shape
    group_tokens, width = contexts.shape
    features = model // n_group
    tokens = group_tokens * n_y * n_core
    z_tokens = own_count * n_xh

    both = jnp.concatenate([contexts, swap(contexts, "xh")], 1)
    row = (y * n_core + core) * n_xh
    own_rows = lax.dynamic_slice_in_dim(weights, (row + xh) * features, features, 0)
    partner_rows = lax.dynamic_slice_in_dim(weights, (row + 1 - xh) * features, features, 0)
    block = jnp.concatenate([own_rows, swap(partner_rows, "xh")], 1)

    spread = upstream.reshape(own_count, n_group, features).transpose(1, 0, 2)
    spread = lax.all_to_all(spread, GROUP, 0, 0, tiled=True)
    spread = spread.reshape(n_group * own_count, features)
    grad_flat = lax.all_gather(spread, "z", axis=0, tiled=True)

    ctx_all = jnp.zeros((n_z, n_y, n_core, z_tokens, 2 * width), BF16)
    for away, piece in ring_gather(both, "y").items():
        there = wrap(y + away, n_y)
        for at, part in ((core, piece), (1 - core, swap(piece, "core"))):
            ctx_all = place(ctx_all, part.reshape(n_z, 1, 1, z_tokens, 2 * width), (0, there, at, 0, 0))
    ctx_flat = ctx_all.reshape(tokens, 2 * width)

    partial_branch = lax.dot_general(
        ctx_flat, block, (((1,), (1,)), ((), ())), preferred_element_type=F32
    ).astype(BF16).reshape(n_z, tokens // n_z, features)
    branch = ring_sum(lambda at: pick(partial_branch, at), z, "z")
    branch = lax.all_to_all(branch.reshape(n_group, own_count, features), GROUP, 0, 0, tiled=True)
    branch = branch.transpose(1, 0, 2).reshape(own_count, model)
    forward = add(residual, branch)
    outgoing = jnp.where(lax.axis_index("section") == 0, forward, upstream)
    received = swap(outgoing, "section")

    partial_ctx = jnp.dot(grad_flat, block, preferred_element_type=F32).astype(BF16)
    partial_ctx = partial_ctx.reshape(n_z, n_y, n_core, z_tokens, 2 * width)
    other = lax.dynamic_index_in_dim(partial_ctx, 1 - core, 2, keepdims=False)
    mine = lax.dynamic_index_in_dim(partial_ctx, core, 2, keepdims=False)
    by_y = add(mine, swap(other, "core"))
    summed = ring_sum(lambda at: lax.dynamic_index_in_dim(by_y, at, 1, keepdims=False), y, "y")
    summed = summed.reshape(group_tokens, 2 * width)
    ctx_grad = add(summed[:, :width], swap(summed[:, width:], "xh"))

    norm_factor = 1.0 / math.sqrt(tokens)
    product = lax.dot_general(grad_flat, ctx_flat, (((0,), (0,)), ((), ())), preferred_element_type=F32)
    product = (norm_factor * product).astype(BF16)
    kept = product[:, :width]
    came = swap(product[:, width:], "xh")
    first = xh == 0
    weight_grad = jnp.concatenate([jnp.where(first, kept, came), jnp.where(first, came, kept)], 0)
    return (forward[None], received[None], ctx_grad[None], weight_grad[None])


def solution(mesh):
    fine = Mesh(mesh.devices.reshape(2, 4, 2, 8, 2), ("section", "y", "core", "z", "xh"))
    tokens = P("section", ("y", "core", "z", "xh"), None)
    heads = P("section", ("y", "core"), ("z", "xh"))
    return jax.shard_map(
        shards,
        mesh=fine,
        in_specs=(tokens, heads, P("section", None, ("z", "xh")), tokens),
        out_specs=(tokens, tokens, heads, heads),
        check_vma=False,
    )
```

```python
import math

import jax
import jax.numpy as jnp
from jax import lax
from jax.sharding import Mesh
from jax.sharding import PartitionSpec as P

BF16 = jnp.bfloat16
F32 = jnp.float32
GROUP = ("y", "core", "xh")


def shift(value, axis, by):
    n = lax.axis_size(axis)
    return lax.ppermute(value, axis, [(i, (i + by) % n) for i in range(n)])


def swap(value, axis):
    return shift(value, axis, 1)


def add(a, b):
    return (a.astype(F32) + b.astype(F32)).astype(BF16)


def wrap(index, n):
    return index & (n - 1)


def pick(stack, index):
    return lax.dynamic_index_in_dim(stack, index, 0, keepdims=False)


def place(buffer, block, starts):
    return lax.dynamic_update_slice(buffer, block, starts)


def tie(*values):
    return lax.optimization_barrier(values)


def both_ways(right, left, axis):
    return shift(right, axis, 1), shift(left, axis, -1)


def shards(segment_input, context, out_proj, grad_output):
    residual = segment_input[0]
    contexts = context[0]
    weights = out_proj[0]
    upstream = grad_output[0]
    section, y, core, z, xh = (lax.axis_index(name) for name in ("section", "y", "core", "z", "xh"))
    n_y, n_core, n_z, n_xh = (lax.axis_size(name) for name in ("y", "core", "z", "xh"))
    n_group = n_y * n_core * n_xh
    own_count, model = upstream.shape
    group_tokens, width = contexts.shape
    features = model // n_group
    tokens = group_tokens * n_y * n_core
    z_tokens = own_count * n_xh
    half = group_tokens // 2
    left_half = features // 2

    spread = upstream.reshape(own_count, n_group, features).transpose(1, 0, 2)
    spread = lax.all_to_all(spread, GROUP, 0, 0, tiled=True).reshape(n_group * own_count, features)
    row = (y * n_core + core) * n_xh
    own_rows = lax.dynamic_slice_in_dim(weights, (row + xh) * features, features, 0)
    partner_rows = lax.dynamic_slice_in_dim(weights, (row + 1 - xh) * features, features, 0)
    both = jnp.concatenate([contexts, swap(contexts, "xh")], 1)

    both, partner_rows = tie(both, partner_rows)
    ctx_left, ctx_right = both_ways(both, both, "y")
    came_rows = swap(partner_rows, "xh")
    block = jnp.concatenate([own_rows, came_rows], 1)

    ctx_left, ctx_right, spread = tie(ctx_left, ctx_right, spread)
    grads = {0: spread}
    grads[-1], grads[1] = both_ways(spread, spread, "z")
    across_low, across_high = both_ways(ctx_left[:half], ctx_right[half:], "y")
    near = swap(jnp.stack([both, ctx_left, ctx_right]), "core")

    grads[-1], grads[1], across_low, across_high, near = tie(grads[-1], grads[1], across_low, across_high, near)
    grads[-2], grads[2] = both_ways(grads[-1], grads[1], "z")
    across = jnp.concatenate([across_low, across_high], 0)
    far = swap(across, "core")
    ctx_all = jnp.zeros((n_z, n_y, n_core, z_tokens, 2 * width), BF16)
    for away, mine, other in ((0, both, near[0]), (-1, ctx_left, near[1]), (1, ctx_right, near[2]), (2, across, far)):
        there = wrap(y + away, n_y)
        for at, part in ((core, mine), (1 - core, other)):
            ctx_all = place(ctx_all, part.reshape(n_z, 1, 1, z_tokens, 2 * width), (0, there, at, 0, 0))
    ctx_flat = ctx_all.reshape(tokens, 2 * width)
    partial_branch = lax.dot_general(
        ctx_flat, block, (((1,), (1,)), ((), ())), preferred_element_type=F32
    ).astype(BF16).reshape(n_z, tokens // n_z, features)

    def chunk(away):
        return pick(partial_branch, wrap(z + away, n_z))

    opposite = chunk(4)
    low, high = opposite[:, :left_half], opposite[:, left_half:]
    grads[-2], grads[2], low, high = tie(grads[-2], grads[2], low, high)
    grads[-3], grads[3] = both_ways(grads[-2], grads[2], "z")
    low, high = both_ways(low, high, "z")
    early = swap(jnp.where(section == 0, residual, upstream), "section")

    grads[-3], grads[3], low, high = tie(grads[-3], grads[3], low, high)
    far_low, far_high = both_ways(grads[-3][:half], grads[3][half:], "z")
    ahead, behind = chunk(3), chunk(-3)
    right = jnp.concatenate([add(ahead[:, :left_half], low), ahead[:, left_half:]], 1)
    left = jnp.concatenate([behind[:, :left_half], add(behind[:, left_half:], high)], 1)
    right, left = both_ways(right, left, "z")

    right, left, far_low, far_high = tie(right, left, far_low, far_high)
    grads[4] = jnp.concatenate([far_low, far_high], 0)
    right, left = both_ways(add(chunk(2), right), add(chunk(-2), left), "z")
    grad_all = jnp.zeros((n_z, tokens // n_z, features), BF16)
    for away, piece in grads.items():
        grad_all = place(grad_all, piece[None], (wrap(z + away, n_z), 0, 0))
    grad_flat = grad_all.reshape(tokens, features)
    partial_ctx = jnp.dot(grad_flat, block, preferred_element_type=F32).astype(BF16)
    partial_ctx = partial_ctx.reshape(n_z, n_y, n_core, z_tokens, 2 * width)
    other_ctx = swap(lax.dynamic_index_in_dim(partial_ctx, 1 - core, 2, keepdims=False), "core")
    norm_factor = 1.0 / math.sqrt(tokens)
    product = lax.dot_general(grad_flat, ctx_flat, (((0,), (0,)), ((), ())), preferred_element_type=F32)
    product = (norm_factor * product).astype(BF16)

    right, left, other_ctx = tie(right, left, other_ctx)
    right, left = both_ways(add(chunk(1), right), add(chunk(-1), left), "z")
    by_y = add(lax.dynamic_index_in_dim(partial_ctx, core, 2, keepdims=False), other_ctx)

    def of_y(away):
        return lax.dynamic_index_in_dim(by_y, wrap(y + away, n_y), 1, keepdims=False).reshape(group_tokens, 2 * width)

    across = of_y(2)
    sum_low, sum_high = both_ways(across[:, :width], across[:, width:], "y")
    came = swap(product[:, width:], "xh")

    right, left, sum_low, sum_high = tie(right, left, sum_low, sum_high)
    own = chunk(0).astype(F32) + right.astype(F32) + left.astype(F32)
    own = own.astype(BF16).reshape(1, n_group, own_count, features)
    sent = jnp.concatenate([own, own], 0).reshape(2 * n_group, own_count, features)
    branch = lax.all_to_all(sent, ("section",) + GROUP, 0, 0, tiled=True)
    ahead, behind = of_y(1), of_y(-1)
    ctx_right = jnp.concatenate([add(ahead[:, :width], sum_low), ahead[:, width:]], 1)
    ctx_left = jnp.concatenate([behind[:, :width], add(behind[:, width:], sum_high)], 1)
    ctx_right, ctx_left = both_ways(ctx_right, ctx_left, "y")
    summed = of_y(0).astype(F32) + ctx_right.astype(F32) + ctx_left.astype(F32)
    ctx_grad = add(summed[:, :width], swap(summed[:, width:].astype(BF16), "xh"))

    branch = branch.reshape(2, n_group, own_count, features).transpose(0, 2, 1, 3).reshape(2, own_count, model)
    forward = add(residual, pick(branch, section))
    received = jnp.where(section == 0, early, add(early, branch[0]))
    kept = product[:, :width]
    first = xh == 0
    weight_grad = jnp.concatenate([jnp.where(first, kept, came), jnp.where(first, came, kept)], 0)
    return (forward[None], received[None], ctx_grad[None], weight_grad[None])


def solution(mesh):
    fine = Mesh(mesh.devices.reshape(2, 4, 2, 8, 2), ("section", "y", "core", "z", "xh"))
    tokens = P("section", ("y", "core", "z", "xh"), None)
    heads = P("section", ("y", "core"), ("z", "xh"))
    return jax.shard_map(
        shards,
        mesh=fine,
        in_specs=(tokens, heads, P("section", None, ("z", "xh")), tokens),
        out_specs=(tokens, tokens, heads, heads),
        check_vma=False,
    )
```

```python
import math

import jax
import jax.numpy as jnp
from jax import lax
from jax.sharding import Mesh
from jax.sharding import PartitionSpec as P

BF16 = jnp.bfloat16
F32 = jnp.float32


def shift(value, axis, by):
    n = lax.axis_size(axis)
    return lax.ppermute(value, axis, [(i, (i + by) % n) for i in range(n)])


def swap(value, axis):
    return shift(value, axis, 1)


def add(a, b):
    return (a.astype(F32) + b.astype(F32)).astype(BF16)


def wrap(index, n):
    return index & (n - 1)


def pick(stack, index, axis=0):
    return lax.dynamic_index_in_dim(stack, index, axis, keepdims=False)


def place(buffer, block, starts):
    return lax.dynamic_update_slice(buffer, block, starts)


def both_ways(right, left, axis):
    return shift(right, axis, 1), shift(left, axis, -1)


def ring_gather(block, axis):
    far = lax.axis_size(axis) // 2
    half = block.shape[0] // 2
    blocks = {0: block}
    right = left = block
    for away in range(1, far):
        right, left = both_ways(right, left, axis)
        blocks[-away], blocks[away] = right, left
    blocks[far] = jnp.concatenate(both_ways(right[:half], left[half:], axis), 0)
    return blocks


def ring_sum(chunk, axis):
    far = lax.axis_size(axis) // 2
    opposite = chunk(far)
    half = opposite.shape[1] // 2
    low, high = both_ways(opposite[:, :half], opposite[:, half:], axis)
    ahead, behind = chunk(far - 1), chunk(1 - far)
    right = jnp.concatenate([add(ahead[:, :half], low), ahead[:, half:]], 1)
    left = jnp.concatenate([behind[:, :half], add(behind[:, half:], high)], 1)
    for away in range(far - 2, 0, -1):
        right, left = both_ways(right, left, axis)
        right, left = add(chunk(away), right), add(chunk(-away), left)
    right, left = both_ways(right, left, axis)
    return chunk(0).astype(F32) + right.astype(F32) + left.astype(F32)


def shards(segment_input, context, out_proj, grad_output):
    residual = segment_input[0]
    contexts = context[0]
    weights = out_proj[0]
    upstream = grad_output[0]
    section, y, core, z, xh = (lax.axis_index(name) for name in ("section", "y", "core", "z", "xh"))
    n_y, n_core, n_z, n_xh = (lax.axis_size(name) for name in ("y", "core", "z", "xh"))
    own_count, model = upstream.shape
    group_tokens, width = contexts.shape
    piece = model // (n_y * n_core * n_xh)
    group = n_y * n_xh
    features = n_core * piece
    tokens = group_tokens * n_y
    z_tokens = own_count * n_xh
    block_tokens = own_count * group

    both = jnp.concatenate([contexts, swap(contexts, "xh")], 1)
    ctx_all = jnp.zeros((n_z, n_y, z_tokens, 2 * width), BF16)
    for away, part in ring_gather(both, "y").items():
        ctx_all = place(ctx_all, part.reshape(n_z, 1, z_tokens, 2 * width), (0, wrap(y + away, n_y), 0, 0))
    ctx_flat = ctx_all.reshape(tokens, 2 * width)

    def rows(core_at, xh_at):
        return lax.dynamic_slice_in_dim(weights, ((y * n_core + core_at) * n_xh + xh_at) * piece, piece, 0)

    came_rows = swap(rows(core, 1 - xh), "xh")
    other_rows = swap(came_rows, "core")
    block = jnp.concatenate(
        [jnp.concatenate([rows(core, xh), came_rows], 1), jnp.concatenate([rows(1 - core, xh), other_rows], 1)], 0
    )

    spread = upstream.reshape(own_count, n_y, n_core, n_xh, piece)
    spread = jnp.stack([pick(spread, core, 2), pick(spread, 1 - core, 2)], 3)
    spread = spread.transpose(1, 2, 0, 3, 4).reshape(group, own_count, features)
    spread = lax.all_to_all(spread, ("y", "xh"), 0, 0, tiled=True).reshape(block_tokens, features)
    grad_all = jnp.zeros((n_z, block_tokens, features), BF16)
    for away, part in ring_gather(spread, "z").items():
        grad_all = place(grad_all, part[None], (wrap(z + away, n_z), 0, 0))
    grad_flat = grad_all.reshape(tokens, features)

    partial_branch = lax.dot_general(
        ctx_flat, block, (((1,), (1,)), ((), ())), preferred_element_type=F32
    ).astype(BF16).reshape(n_z, block_tokens, features)
    branch = ring_sum(lambda away: pick(partial_branch, wrap(z + away, n_z)), "z").astype(BF16)
    branch = branch.reshape(1, group, own_count, features)
    branch = jnp.concatenate([branch, branch], 0).reshape(2 * group, own_count, features)
    branch = lax.all_to_all(branch, ("section", "y", "xh"), 0, 0, tiled=True)
    branch = branch.reshape(2, n_y, n_xh, own_count, n_core, piece)
    branch = jnp.where(core == 0, branch, jnp.flip(branch, 4))
    branch = branch.transpose(0, 3, 1, 4, 2, 5).reshape(2, own_count, model)
    forward = add(residual, pick(branch, section))
    early = swap(jnp.where(section == 0, residual, upstream), "section")
    received = jnp.where(section == 0, early, add(early, branch[0]))

    partial_ctx = jnp.dot(grad_flat, block, preferred_element_type=F32).astype(BF16)
    partial_ctx = partial_ctx.reshape(n_z, n_y, z_tokens, 2 * width)
    summed = ring_sum(lambda away: pick(partial_ctx, wrap(y + away, n_y), 1).reshape(group_tokens, 2 * width), "y")
    ctx_grad = add(summed[:, :width], swap(summed[:, width:].astype(BF16), "xh"))

    norm_factor = 1.0 / math.sqrt(tokens * n_core)
    product = lax.dot_general(grad_flat, ctx_flat, (((0,), (0,)), ((), ())), preferred_element_type=F32)
    product = (norm_factor * product).astype(BF16)
    own_rows = add(product[:piece], swap(product[piece:], "core"))
    kept = own_rows[:, :width]
    came = swap(own_rows[:, width:], "xh")
    first = xh == 0
    weight_grad = jnp.concatenate([jnp.where(first, kept, came), jnp.where(first, came, kept)], 0)
    return (forward[None], received[None], ctx_grad[None], weight_grad[None])


def solution(mesh):
    fine = Mesh(mesh.devices.reshape(2, 4, 2, 8, 2), ("section", "y", "core", "z", "xh"))
    tokens = P("section", ("y", "core", "z", "xh"), None)
    heads = P("section", ("y", "core"), ("z", "xh"))
    return jax.shard_map(
        shards,
        mesh=fine,
        in_specs=(tokens, heads, P("section", None, ("z", "xh")), tokens),
        out_specs=(tokens, tokens, heads, heads),
        check_vma=False,
    )
```

```python
import math

import jax
import jax.numpy as jnp
from jax import lax
from jax.sharding import Mesh
from jax.sharding import PartitionSpec as P

BF16 = jnp.bfloat16
F32 = jnp.float32


def shift(value, axis, by):
    n = lax.axis_size(axis)
    return lax.ppermute(value, axis, [(i, (i + by) % n) for i in range(n)])


def swap(value, axis):
    return shift(value, axis, 1)


def add(a, b):
    return (a.astype(F32) + b.astype(F32)).astype(BF16)


def wrap(index, n):
    return index & (n - 1)


def pick(stack, index, axis=0):
    return lax.dynamic_index_in_dim(stack, index, axis, keepdims=False)


def place(buffer, block, starts):
    return lax.dynamic_update_slice(buffer, block, starts)


def tie(*values):
    return lax.optimization_barrier(values)


def both_ways(right, left, axis):
    return shift(right, axis, 1), shift(left, axis, -1)


def ring_gather(block, axis):
    far = lax.axis_size(axis) // 2
    half = block.shape[0] // 2
    blocks = {0: block}
    right = left = block
    for away in range(1, far):
        right, left = both_ways(right, left, axis)
        blocks[-away], blocks[away] = right, left
    return blocks, both_ways(right[:half], left[half:], axis)


def ring_steps(chunk, axis):
    far = lax.axis_size(axis) // 2
    opposite = chunk(far)
    half = opposite.shape[1] // 2
    low, high = yield both_ways(opposite[:, :half], opposite[:, half:], axis)
    ahead, behind = chunk(far - 1), chunk(1 - far)
    right = jnp.concatenate([add(ahead[:, :half], low), ahead[:, half:]], 1)
    left = jnp.concatenate([behind[:, :half], add(behind[:, half:], high)], 1)
    for away in range(far - 2, 0, -1):
        right, left = yield both_ways(right, left, axis)
        right, left = add(chunk(away), right), add(chunk(-away), left)
    right, left = yield both_ways(right, left, axis)
    yield chunk(0).astype(F32) + right.astype(F32) + left.astype(F32)


def shards(segment_input, context, out_proj, grad_output):
    residual = segment_input[0]
    contexts = context[0]
    weights = out_proj[0]
    upstream = grad_output[0]
    section, y, core, z, xh = (lax.axis_index(name) for name in ("section", "y", "core", "z", "xh"))
    n_y, n_core, n_z, n_xh = (lax.axis_size(name) for name in ("y", "core", "z", "xh"))
    own_count, model = upstream.shape
    group_tokens, width = contexts.shape
    piece = model // (n_y * n_core * n_xh)
    group = n_y * n_xh
    features = n_core * piece
    tokens = group_tokens * n_y
    z_tokens = own_count * n_xh
    block_tokens = own_count * group

    both = jnp.concatenate([contexts, swap(contexts, "xh")], 1)
    def rows(core_at, xh_at):
        return lax.dynamic_slice_in_dim(weights, ((y * n_core + core_at) * n_xh + xh_at) * piece, piece, 0)

    both, partner_rows = tie(both, rows(core, 1 - xh))
    came_rows = swap(partner_rows, "xh")
    other_rows = swap(came_rows, "core")
    outgoing, came_rows = tie(jnp.where(section == 0, residual, upstream), came_rows)
    early = swap(outgoing, "section")
    block = jnp.concatenate(
        [jnp.concatenate([rows(core, xh), came_rows], 1), jnp.concatenate([rows(1 - core, xh), other_rows], 1)], 0
    )

    ctx_all = jnp.zeros((n_z, n_y, z_tokens, 2 * width), BF16)
    ctx_blocks, across = ring_gather(both, "y")
    ctx_blocks[n_y // 2] = jnp.concatenate(across, 0)
    for away, part in ctx_blocks.items():
        ctx_all = place(ctx_all, part.reshape(n_z, 1, z_tokens, 2 * width), (0, wrap(y + away, n_y), 0, 0))
    ctx_flat = ctx_all.reshape(tokens, 2 * width)

    spread = upstream.reshape(own_count, n_y, n_core, n_xh, piece)
    spread = jnp.stack([pick(spread, core, 2), pick(spread, 1 - core, 2)], 3)
    spread = spread.transpose(1, 2, 0, 3, 4).reshape(group, own_count, features)
    spread = lax.all_to_all(spread, ("y", "xh"), 0, 0, tiled=True).reshape(block_tokens, features)
    grad_all = jnp.zeros((n_z, block_tokens, features), BF16)
    grad_blocks, far_blocks = ring_gather(spread, "z")
    for away, part in grad_blocks.items():
        grad_all = place(grad_all, part[None], (wrap(z + away, n_z), 0, 0))

    partial_branch = lax.dot_general(
        ctx_flat, block, (((1,), (1,)), ((), ())), preferred_element_type=F32
    ).astype(BF16).reshape(n_z, block_tokens, features)
    ring = ring_steps(lambda away: pick(partial_branch, wrap(z + away, n_z)), "z")
    *step, early = tie(*next(ring), early)
    step = ring.send(step)
    *step, far_low, far_high = tie(*step, *far_blocks)
    step = ring.send(step)
    grad_all = place(grad_all, jnp.concatenate([far_low, far_high], 0)[None], (wrap(z + n_z // 2, n_z), 0, 0))
    grad_flat = grad_all.reshape(tokens, features)
    partial_ctx = jnp.dot(grad_flat, block, preferred_element_type=F32).astype(BF16)
    norm_factor = 1.0 / math.sqrt(tokens * n_core)
    product = lax.dot_general(grad_flat, ctx_flat, (((0,), (0,)), ((), ())), preferred_element_type=F32)
    product = (norm_factor * product).astype(BF16)
    *step, partial_ctx, product = tie(*step, partial_ctx, product)
    step = ring.send(step)
    partial_ctx = partial_ctx.reshape(n_z, n_y, z_tokens, 2 * width)
    ctx_ring = ring_steps(lambda away: pick(partial_ctx, wrap(y + away, n_y), 1).reshape(group_tokens, 2 * width), "y")
    ctx_step = next(ctx_ring)
    *step, ctx_low, ctx_high, product = tie(*step, *ctx_step, product)
    branch = ring.send(step).astype(BF16)
    branch = branch.reshape(1, group, own_count, features)
    branch = jnp.concatenate([branch, branch], 0).reshape(2 * group, own_count, features)
    branch = lax.all_to_all(branch, ("section", "y", "xh"), 0, 0, tiled=True)
    branch = branch.reshape(2, n_y, n_xh, own_count, n_core, piece)
    branch = jnp.where(core == 0, branch, jnp.flip(branch, 4))
    branch = branch.transpose(0, 3, 1, 4, 2, 5).reshape(2, own_count, model)
    forward = add(residual, pick(branch, section))
    received = jnp.where(section == 0, early, add(early, branch[0]))

    summed = ctx_ring.send(ctx_ring.send((ctx_low, ctx_high)))
    ctx_grad = add(summed[:, :width], swap(summed[:, width:].astype(BF16), "xh"))

    own_rows = add(product[:piece], swap(product[piece:], "core"))
    kept = own_rows[:, :width]
    came = swap(own_rows[:, width:], "xh")
    first = xh == 0
    weight_grad = jnp.concatenate([jnp.where(first, kept, came), jnp.where(first, came, kept)], 0)
    return (forward[None], received[None], ctx_grad[None], weight_grad[None])


def solution(mesh):
    fine = Mesh(mesh.devices.reshape(2, 4, 2, 8, 2), ("section", "y", "core", "z", "xh"))
    tokens = P("section", ("y", "core", "z", "xh"), None)
    heads = P("section", ("y", "core"), ("z", "xh"))
    return jax.shard_map(
        shards,
        mesh=fine,
        in_specs=(tokens, heads, P("section", None, ("z", "xh")), tokens),
        out_specs=(tokens, tokens, heads, heads),
        check_vma=False,
    )
```

```python
import math

import jax
import jax.numpy as jnp
from jax import lax
from jax.sharding import Mesh
from jax.sharding import PartitionSpec as P

BF16 = jnp.bfloat16
F32 = jnp.float32


def shift(value, axis, by):
    n = lax.axis_size(axis)
    return lax.ppermute(value, axis, [(i, (i + by) % n) for i in range(n)])


def swap(value, axis):
    return shift(value, axis, 1)


def add(a, b):
    return (a.astype(F32) + b.astype(F32)).astype(BF16)


def wrap(index, n):
    return index & (n - 1)


def pick(stack, index, axis=0):
    return lax.dynamic_index_in_dim(stack, index, axis, keepdims=False)


def place(buffer, block, starts):
    return lax.dynamic_update_slice(buffer, block, starts)


def tie(*values):
    return lax.optimization_barrier(values)


def both_ways(right, left, axis):
    return shift(right, axis, 1), shift(left, axis, -1)


def ring_gather(block, axis):
    far = lax.axis_size(axis) // 2
    half = block.shape[0] // 2
    blocks = {0: block}
    right = left = block
    for away in range(1, far):
        right, left = both_ways(right, left, axis)
        blocks[-away], blocks[away] = right, left
    return blocks, both_ways(right[:half], left[half:], axis)


def ring_steps(chunk, axis):
    far = lax.axis_size(axis) // 2
    opposite = chunk(far)
    half = opposite.shape[1] // 2
    low, high = yield both_ways(opposite[:, :half], opposite[:, half:], axis)
    ahead, behind = chunk(far - 1), chunk(1 - far)
    right = jnp.concatenate([add(ahead[:, :half], low), ahead[:, half:]], 1)
    left = jnp.concatenate([behind[:, :half], add(behind[:, half:], high)], 1)
    for away in range(far - 2, 0, -1):
        right, left = yield both_ways(right, left, axis)
        right, left = add(chunk(away), right), add(chunk(-away), left)
    right, left = yield both_ways(right, left, axis)
    yield chunk(0).astype(F32) + right.astype(F32) + left.astype(F32)


def shards(segment_input, context, out_proj, grad_output):
    residual = segment_input[0]
    contexts = context[0]
    weights = out_proj[0]
    upstream = grad_output[0]
    section, y, core, z, xh = (lax.axis_index(name) for name in ("section", "y", "core", "z", "xh"))
    n_y, n_core, n_z, n_xh = (lax.axis_size(name) for name in ("y", "core", "z", "xh"))
    own_count, model = upstream.shape
    group_tokens, width = contexts.shape
    piece = model // (n_y * n_core * n_xh)
    group = n_y * n_xh
    tokens = group_tokens * n_y
    z_tokens = own_count * n_xh
    block_tokens = own_count * group

    both = jnp.concatenate([contexts, swap(contexts, "xh")], 1)
    def rows(core_at, xh_at):
        return lax.dynamic_slice_in_dim(weights, ((y * n_core + core_at) * n_xh + xh_at) * piece, piece, 0)

    both, partner_rows = tie(both, rows(core, 1 - xh))
    came_rows = swap(partner_rows, "xh")
    other_rows = swap(came_rows, "core")
    outgoing, came_rows = tie(jnp.where(section == 0, residual, upstream), came_rows)
    early = swap(outgoing, "section")
    own_block = jnp.concatenate([rows(core, xh), came_rows], 1)
    other_block = jnp.concatenate([rows(1 - core, xh), other_rows], 1)

    ctx_all = jnp.zeros((n_z, n_y, z_tokens, 2 * width), BF16)
    ctx_blocks, across = ring_gather(both, "y")
    ctx_blocks[n_y // 2] = jnp.concatenate(across, 0)
    for away, part in ctx_blocks.items():
        ctx_all = place(ctx_all, part.reshape(n_z, 1, z_tokens, 2 * width), (0, wrap(y + away, n_y), 0, 0))
    ctx_flat = ctx_all.reshape(tokens, 2 * width)

    spread = upstream.reshape(own_count, n_y, n_core, n_xh, piece)
    spread = jnp.stack([pick(spread, core, 2), pick(spread, 1 - core, 2)], 3)
    spread = spread.transpose(1, 2, 3, 0, 4).reshape(group, n_core, own_count, piece)
    spread = lax.all_to_all(spread, ("y", "xh"), 0, 0, tiled=True)
    own_spread = spread[:, 0].reshape(block_tokens, piece)
    other_spread = spread[:, 1].reshape(block_tokens, piece)

    other_grad = lax.all_gather(other_spread, "z", axis=0, tiled=True)
    grad_blocks, far_blocks = ring_gather(own_spread, "z")
    own_grad = jnp.zeros((n_z, block_tokens, piece), BF16)
    for away, part in grad_blocks.items():
        own_grad = place(own_grad, part[None], (wrap(z + away, n_z), 0, 0))

    def of_context(rows_of):
        return lax.dot_general(ctx_flat, rows_of, (((1,), (1,)), ((), ())), preferred_element_type=F32).astype(BF16)

    own_partial = of_context(own_block).reshape(n_z, block_tokens, piece)
    other_partial = of_context(other_block)
    ring = ring_steps(lambda away: pick(own_partial, wrap(z + away, n_z)), "z")
    *step, early = tie(*next(ring), early)
    step = ring.send(step)
    *step, far_low, far_high, other_grad = tie(*step, *far_blocks, other_grad)
    other_branch = lax.psum_scatter(other_partial, "z", scatter_dimension=0, tiled=True)
    step = ring.send(step)
    own_grad = place(own_grad, jnp.concatenate([far_low, far_high], 0)[None], (wrap(z + n_z // 2, n_z), 0, 0))
    own_grad = own_grad.reshape(tokens, piece)
    partial_ctx = (
        jnp.dot(other_grad, other_block, preferred_element_type=F32)
        + jnp.dot(own_grad, own_block, preferred_element_type=F32)
    ).astype(BF16)
    norm_factor = 1.0 / math.sqrt(tokens * n_core)

    def of_gradient(grad):
        product = lax.dot_general(grad, ctx_flat, (((0,), (0,)), ((), ())), preferred_element_type=F32)
        return (norm_factor * product).astype(BF16)

    other_product = swap(of_gradient(other_grad), "core")
    own_product = of_gradient(own_grad)
    *step, partial_ctx, own_product = tie(*step, partial_ctx, own_product)
    step = ring.send(step)
    partial_ctx = partial_ctx.reshape(n_z, n_y, z_tokens, 2 * width)
    ctx_ring = ring_steps(lambda away: pick(partial_ctx, wrap(y + away, n_y), 1).reshape(group_tokens, 2 * width), "y")
    ctx_step = next(ctx_ring)
    *step, ctx_low, ctx_high, other_product = tie(*step, *ctx_step, other_product)
    own_branch = ring.send(step).astype(BF16)
    branch = jnp.stack([own_branch.reshape(group, own_count, piece), other_branch.reshape(group, own_count, piece)], 1)
    branch = jnp.concatenate([branch, branch], 0)
    branch = lax.all_to_all(branch, ("section", "y", "xh"), 0, 0, tiled=True)
    branch = branch.reshape(2, n_y, n_xh, n_core, own_count, piece)
    branch = jnp.where(core == 0, branch, jnp.flip(branch, 3))
    branch = branch.transpose(0, 4, 1, 3, 2, 5).reshape(2, own_count, model)
    forward = add(residual, pick(branch, section))
    received = jnp.where(section == 0, early, add(early, branch[0]))

    summed = ctx_ring.send(ctx_ring.send((ctx_low, ctx_high)))
    ctx_grad = add(summed[:, :width], swap(summed[:, width:].astype(BF16), "xh"))

    own_rows = add(own_product, other_product)
    kept = own_rows[:, :width]
    came = swap(own_rows[:, width:], "xh")
    first = xh == 0
    weight_grad = jnp.concatenate([jnp.where(first, kept, came), jnp.where(first, came, kept)], 0)
    return (forward[None], received[None], ctx_grad[None], weight_grad[None])


def solution(mesh):
    fine = Mesh(mesh.devices.reshape(2, 4, 2, 8, 2), ("section", "y", "core", "z", "xh"))
    tokens = P("section", ("y", "core", "z", "xh"), None)
    heads = P("section", ("y", "core"), ("z", "xh"))
    return jax.shard_map(
        shards,
        mesh=fine,
        in_specs=(tokens, heads, P("section", None, ("z", "xh")), tokens),
        out_specs=(tokens, tokens, heads, heads),
        check_vma=False,
    )
```

```python
import functools
import math

import jax
import jax.numpy as jnp
from jax import lax
from jax.experimental import pallas as pl
from jax.experimental.pallas import tpu as pltpu
from jax.sharding import Mesh
from jax.sharding import PartitionSpec as P

BF16 = jnp.bfloat16
F32 = jnp.float32


def shift(value, axis, by):
    n = lax.axis_size(axis)
    return lax.ppermute(value, axis, [(i, (i + by) % n) for i in range(n)])


def swap(value, axis):
    return shift(value, axis, 1)


def add(a, b):
    return (a.astype(F32) + b.astype(F32)).astype(BF16)


def wrap(index, n):
    return index & (n - 1)


def pick(stack, index, axis=0):
    return lax.dynamic_index_in_dim(stack, index, axis, keepdims=False)


def place(buffer, block, starts):
    return lax.dynamic_update_slice(buffer, block, starts)


def tie(*values):
    return lax.optimization_barrier(values)


def both_ways(right, left, axis):
    return shift(right, axis, 1), shift(left, axis, -1)


def ring_gather(block, axis):
    far = lax.axis_size(axis) // 2
    half = block.shape[0] // 2
    blocks = {0: block}
    right = left = block
    for away in range(1, far):
        right, left = both_ways(right, left, axis)
        blocks[-away], blocks[away] = right, left
    return blocks, both_ways(right[:half], left[half:], axis)


def ring_steps(chunk, axis):
    far = lax.axis_size(axis) // 2
    opposite = chunk(far)
    half = opposite.shape[1] // 2
    low, high = yield both_ways(opposite[:, :half], opposite[:, half:], axis)
    ahead, behind = chunk(far - 1), chunk(1 - far)
    right = jnp.concatenate([add(ahead[:, :half], low), ahead[:, half:]], 1)
    left = jnp.concatenate([behind[:, :half], add(behind[:, half:], high)], 1)
    for away in range(far - 2, 0, -1):
        right, left = yield both_ways(right, left, axis)
        right, left = add(chunk(away), right), add(chunk(-away), left)
    right, left = yield both_ways(right, left, axis)
    yield chunk(0).astype(F32) + right.astype(F32) + left.astype(F32)


def by_group(n_y, n_core, n_xh, piece):
    for y in range(n_y):
        for xh in range(n_xh):
            for core in range(n_core):
                yield y * n_xh + xh, core, ((y * n_core + core) * n_xh + xh) * piece


def spread_kernel(sizes, at_ref, rows_ref, out_ref):
    piece = sizes[-1]
    core = at_ref[1]
    pieces = {(group, at): rows_ref[:, first : first + piece] for group, at, first in by_group(*sizes)}
    for group, at in pieces:
        chosen = jnp.where(core == 0, pieces[group, at], pieces[group, 1 - at])
        out_ref[group, :, at * piece : (at + 1) * piece] = chosen


def finish_kernel(sizes, at_ref, branch_ref, residual_ref, early_ref, forward_ref, received_ref):
    piece = sizes[-1]
    section, core = at_ref[0], at_ref[1]
    for group, at, first in by_group(*sizes):
        here = slice(first, first + piece)

        def term(of_section):
            mine, other = branch_ref[of_section, group, :, :piece], branch_ref[of_section, group, :, piece:]
            return jnp.where(core == at, mine, other).astype(F32)

        one, two = term(0), term(1)
        forward_ref[:, here] = (residual_ref[:, here].astype(F32) + jnp.where(section == 0, one, two)).astype(BF16)
        early = early_ref[:, here]
        received_ref[:, here] = jnp.where(section == 0, early, (early.astype(F32) + one).astype(BF16))


def send_kernel(at_ref, context_ref, weights_ref, out_ref, done):
    count, height = context_ref.shape[0], out_ref.shape[0] - context_ref.shape[0]
    row = pl.multiple_of(at_ref[2] * height, height)
    copies = [
        pltpu.make_async_copy(context_ref, out_ref.at[:count], done.at[0]),
        pltpu.make_async_copy(weights_ref.at[pl.ds(row, height)], out_ref.at[count:], done.at[1]),
    ]
    for copy in copies:
        copy.start()
    for copy in copies:
        copy.wait()


def local(kernel, at, arrays, shapes):
    whole = pl.BlockSpec(memory_space=pltpu.VMEM)
    return pl.pallas_call(
        kernel,
        out_shape=[jax.ShapeDtypeStruct(shape, BF16) for shape in shapes],
        in_specs=[pl.BlockSpec(memory_space=pltpu.SMEM)] + [whole] * len(arrays),
        out_specs=[whole] * len(shapes),
        compiler_params=pltpu.CompilerParams(vmem_limit_bytes=24 * 2**20),
    )(at, *arrays)


def shards(segment_input, context, out_proj, grad_output):
    residual = segment_input[0]
    contexts = context[0]
    weights = out_proj[0]
    upstream = grad_output[0]
    section, y, core, z, xh = (lax.axis_index(name) for name in ("section", "y", "core", "z", "xh"))
    n_y, n_core, n_z, n_xh = (lax.axis_size(name) for name in ("y", "core", "z", "xh"))
    own_count, model = upstream.shape
    group_tokens, width = contexts.shape
    piece = model // (n_y * n_core * n_xh)
    group = n_y * n_xh
    features = n_core * piece
    tokens = group_tokens * n_y
    z_tokens = own_count * n_xh
    block_tokens = own_count * group
    sizes = (n_y, n_core, n_xh, piece)
    block_at = (y * n_core + core) * n_xh
    at = jnp.stack([section, core, block_at + 1 - xh]).astype(jnp.int32)

    def rows(core_at, xh_at):
        return lax.dynamic_slice_in_dim(weights, ((y * n_core + core_at) * n_xh + xh_at) * piece, piece, 0)

    anywhere = pl.BlockSpec(memory_space=pl.ANY)
    sent = pl.pallas_call(
        send_kernel,
        out_shape=jax.ShapeDtypeStruct((group_tokens + piece, width), BF16),
        in_specs=[pl.BlockSpec(memory_space=pltpu.SMEM), anywhere, anywhere],
        out_specs=anywhere,
        scratch_shapes=[pltpu.SemaphoreType.DMA((2,))],
    )(at, contexts, weights)
    came = swap(sent, "xh")

    (spread,) = local(functools.partial(spread_kernel, sizes), at, [upstream], [(group, own_count, features)])
    spread = lax.all_to_all(spread, ("y", "xh"), 0, 0, tiled=True).reshape(block_tokens, features)
    spread, came = tie(spread, came)
    both = jnp.concatenate([contexts, came[:group_tokens]], 1)
    came_rows = came[group_tokens:]

    other_rows = swap(came_rows, "core")
    block = jnp.concatenate(
        [jnp.concatenate([rows(core, xh), came_rows], 1), jnp.concatenate([rows(1 - core, xh), other_rows], 1)], 0
    )

    ctx_blocks, across = ring_gather(both, "y")
    ctx_blocks[n_y // 2] = jnp.concatenate(across, 0)
    ctx_all = jnp.zeros((n_z, n_y, z_tokens, 2 * width), BF16)
    for away, part in ctx_blocks.items():
        ctx_all = place(ctx_all, part.reshape(n_z, 1, z_tokens, 2 * width), (0, wrap(y + away, n_y), 0, 0))
    ctx_flat = ctx_all.reshape(tokens, 2 * width)

    grad_blocks, far_blocks = ring_gather(spread, "z")
    grad_all = jnp.zeros((n_z, block_tokens, features), BF16)
    for away, part in grad_blocks.items():
        grad_all = place(grad_all, part[None], (wrap(z + away, n_z), 0, 0))

    partial_branch = lax.dot_general(
        ctx_flat, block, (((1,), (1,)), ((), ())), preferred_element_type=F32
    ).astype(BF16).reshape(n_z, block_tokens, features)
    ring = ring_steps(lambda away: pick(partial_branch, wrap(z + away, n_z)), "z")
    *step, outgoing = tie(*next(ring), jnp.where(section == 0, residual, upstream))
    early = swap(outgoing, "section")
    step = ring.send(step)
    *step, far_low, far_high = tie(*step, *far_blocks)
    step = ring.send(step)
    grad_all = place(grad_all, jnp.concatenate([far_low, far_high], 0)[None], (wrap(z + n_z // 2, n_z), 0, 0))
    grad_flat = grad_all.reshape(tokens, features)
    norm_factor = 1.0 / math.sqrt(tokens * n_core)
    product = lax.dot_general(grad_flat, ctx_flat, (((0,), (0,)), ((), ())), preferred_element_type=F32)
    product = (norm_factor * product).astype(BF16)
    partial_ctx = jnp.dot(grad_flat, block, preferred_element_type=F32).astype(BF16)
    *step, partial_ctx, product, early = tie(*step, partial_ctx, product, early)
    other_product = swap(product[piece:], "core")
    step = ring.send(step)
    partial_ctx = partial_ctx.reshape(n_z, n_y, z_tokens, 2 * width)
    ctx_ring = ring_steps(lambda away: pick(partial_ctx, wrap(y + away, n_y), 1).reshape(group_tokens, 2 * width), "y")
    ctx_step = next(ctx_ring)
    ctx_low, ctx_high, other_product = tie(*ctx_step, other_product)
    branch = ring.send(step).astype(BF16)
    branch = branch.reshape(1, group, own_count, features)
    branch = jnp.concatenate([branch, branch], 0).reshape(2 * group, own_count, features)
    branch = lax.all_to_all(branch, ("section", "y", "xh"), 0, 0, tiled=True)

    summed = ctx_ring.send(ctx_ring.send((ctx_low, ctx_high)))
    branch, summed = tie(branch, summed)
    ctx_grad = add(summed[:, :width], swap(summed[:, width:].astype(BF16), "xh"))
    forward, received = local(
        functools.partial(finish_kernel, sizes),
        at,
        [branch.reshape(2, group, own_count, features), residual, early],
        [residual.shape, residual.shape],
    )

    own_rows = add(product[:piece], other_product)
    kept = own_rows[:, :width]
    came = swap(own_rows[:, width:], "xh")
    first = xh == 0
    weight_grad = jnp.concatenate([jnp.where(first, kept, came), jnp.where(first, came, kept)], 0)
    return (forward[None], received[None], ctx_grad[None], weight_grad[None])


def solution(mesh):
    fine = Mesh(mesh.devices.reshape(2, 4, 2, 8, 2), ("section", "y", "core", "z", "xh"))
    tokens = P("section", ("y", "core", "z", "xh"), None)
    heads = P("section", ("y", "core"), ("z", "xh"))
    return jax.shard_map(
        shards,
        mesh=fine,
        in_specs=(tokens, heads, P("section", None, ("z", "xh")), tokens),
        out_specs=(tokens, tokens, heads, heads),
        check_vma=False,
    )
```

```python
import functools
import math

import jax
import jax.numpy as jnp
from jax import lax
from jax.experimental import pallas as pl
from jax.experimental.pallas import tpu as pltpu
from jax.sharding import Mesh
from jax.sharding import PartitionSpec as P

BF16 = jnp.bfloat16
F32 = jnp.float32


def shift(value, axis, by):
    n = lax.axis_size(axis)
    return lax.ppermute(value, axis, [(i, (i + by) % n) for i in range(n)])


def swap(value, axis):
    return shift(value, axis, 1)


def add(a, b):
    return (a.astype(F32) + b.astype(F32)).astype(BF16)


def wrap(index, n):
    return index & (n - 1)


def pick(stack, index, axis=0):
    return lax.dynamic_index_in_dim(stack, index, axis, keepdims=False)


def place(buffer, block, starts):
    return lax.dynamic_update_slice(buffer, block, starts)


def tie(*values):
    return lax.optimization_barrier(values)


def both_ways(right, left, axis):
    return shift(right, axis, 1), shift(left, axis, -1)


def ring_gather(block, axis):
    far = lax.axis_size(axis) // 2
    half = block.shape[0] // 2
    blocks = {0: block}
    right = left = block
    for away in range(1, far):
        right, left = both_ways(right, left, axis)
        blocks[-away], blocks[away] = right, left
    return blocks, both_ways(right[:half], left[half:], axis)


def ring_steps(chunk, axis):
    far = lax.axis_size(axis) // 2
    opposite = chunk(far)
    half = opposite.shape[1] // 2
    low, high = yield both_ways(opposite[:, :half], opposite[:, half:], axis)
    ahead, behind = chunk(far - 1), chunk(1 - far)
    right = jnp.concatenate([add(ahead[:, :half], low), ahead[:, half:]], 1)
    left = jnp.concatenate([behind[:, :half], add(behind[:, half:], high)], 1)
    for away in range(far - 2, 0, -1):
        right, left = yield both_ways(right, left, axis)
        right, left = add(chunk(away), right), add(chunk(-away), left)
    right, left = yield both_ways(right, left, axis)
    yield chunk(0).astype(F32) + right.astype(F32) + left.astype(F32)


def by_group(n_y, n_core, n_xh, piece):
    for y in range(n_y):
        for xh in range(n_xh):
            for core in range(n_core):
                yield y * n_xh + xh, core, ((y * n_core + core) * n_xh + xh) * piece


def spread_kernel(sizes, at_ref, rows_ref, out_ref):
    piece = sizes[-1]
    core = at_ref[1]
    pieces = {(group, at): rows_ref[:, first : first + piece] for group, at, first in by_group(*sizes)}
    for group, at in pieces:
        chosen = jnp.where(core == 0, pieces[group, at], pieces[group, 1 - at])
        out_ref[group, :, at * piece : (at + 1) * piece] = chosen


def finish_kernel(sizes, at_ref, branch_ref, residual_ref, early_ref, forward_ref, received_ref):
    piece = sizes[-1]
    section, core = at_ref[0], at_ref[1]
    for group, at, first in by_group(*sizes):
        here = slice(first, first + piece)

        def term(of_section):
            mine, other = branch_ref[of_section, group, :, :piece], branch_ref[of_section, group, :, piece:]
            return jnp.where(core == at, mine, other).astype(F32)

        one, two = term(0), term(1)
        forward_ref[:, here] = (residual_ref[:, here].astype(F32) + jnp.where(section == 0, one, two)).astype(BF16)
        early = early_ref[:, here]
        received_ref[:, here] = jnp.where(section == 0, early, (early.astype(F32) + one).astype(BF16))


def local(kernel, at, arrays, shapes):
    whole = pl.BlockSpec(memory_space=pltpu.VMEM)
    return pl.pallas_call(
        kernel,
        out_shape=[jax.ShapeDtypeStruct(shape, BF16) for shape in shapes],
        in_specs=[pl.BlockSpec(memory_space=pltpu.SMEM)] + [whole] * len(arrays),
        out_specs=[whole] * len(shapes),
        compiler_params=pltpu.CompilerParams(vmem_limit_bytes=24 * 2**20),
    )(at, *arrays)


def shards(segment_input, context, out_proj, grad_output):
    residual = segment_input[0]
    contexts = context[0]
    weights = out_proj[0]
    upstream = grad_output[0]
    section, y, core, z, xh = (lax.axis_index(name) for name in ("section", "y", "core", "z", "xh"))
    n_y, n_core, n_z, n_xh = (lax.axis_size(name) for name in ("y", "core", "z", "xh"))
    own_count, model = upstream.shape
    group_tokens, width = contexts.shape
    piece = model // (n_y * n_core * n_xh)
    group = n_y * n_xh
    features = n_core * piece
    tokens = group_tokens * n_y
    z_tokens = own_count * n_xh
    block_tokens = own_count * group

    both = jnp.concatenate([contexts, swap(contexts, "xh")], 1)
    def rows(core_at, xh_at):
        return lax.dynamic_slice_in_dim(weights, ((y * n_core + core_at) * n_xh + xh_at) * piece, piece, 0)

    both, partner_rows = tie(both, rows(core, 1 - xh))
    came_rows = swap(partner_rows, "xh")
    other_rows = swap(came_rows, "core")
    outgoing, came_rows = tie(jnp.where(section == 0, residual, upstream), came_rows)
    early = swap(outgoing, "section")
    block = jnp.concatenate(
        [jnp.concatenate([rows(core, xh), came_rows], 1), jnp.concatenate([rows(1 - core, xh), other_rows], 1)], 0
    )

    ctx_all = jnp.zeros((n_z, n_y, z_tokens, 2 * width), BF16)
    ctx_blocks, across = ring_gather(both, "y")
    ctx_blocks[n_y // 2] = jnp.concatenate(across, 0)
    for away, part in ctx_blocks.items():
        ctx_all = place(ctx_all, part.reshape(n_z, 1, z_tokens, 2 * width), (0, wrap(y + away, n_y), 0, 0))
    ctx_flat = ctx_all.reshape(tokens, 2 * width)

    sizes = (n_y, n_core, n_xh, piece)
    at = jnp.stack([section, core]).astype(jnp.int32)
    (spread,) = local(functools.partial(spread_kernel, sizes), at, [upstream], [(group, own_count, features)])
    spread = lax.all_to_all(spread, ("y", "xh"), 0, 0, tiled=True).reshape(block_tokens, features)
    grad_all = jnp.zeros((n_z, block_tokens, features), BF16)
    grad_blocks, far_blocks = ring_gather(spread, "z")
    for away, part in grad_blocks.items():
        grad_all = place(grad_all, part[None], (wrap(z + away, n_z), 0, 0))

    partial_branch = lax.dot_general(
        ctx_flat, block, (((1,), (1,)), ((), ())), preferred_element_type=F32
    ).astype(BF16).reshape(n_z, block_tokens, features)
    ring = ring_steps(lambda away: pick(partial_branch, wrap(z + away, n_z)), "z")
    *step, early = tie(*next(ring), early)
    step = ring.send(step)
    far = jnp.concatenate(far_blocks, 0)[None]
    grad_flat = place(grad_all, far, (wrap(z + n_z // 2, n_z), 0, 0)).reshape(tokens, features)
    partial_ctx = jnp.dot(grad_flat, block, preferred_element_type=F32).astype(BF16)
    *step, partial_ctx = tie(*step, partial_ctx)
    step = ring.send(step)
    norm_factor = 1.0 / math.sqrt(tokens * n_core)
    product = lax.dot_general(grad_flat, ctx_flat, (((0,), (0,)), ((), ())), preferred_element_type=F32)
    product, partial_ctx = tie((norm_factor * product).astype(BF16), partial_ctx)
    partial_ctx = partial_ctx.reshape(n_z, n_y, z_tokens, 2 * width)
    ctx_ring = ring_steps(lambda away: pick(partial_ctx, wrap(y + away, n_y), 1).reshape(group_tokens, 2 * width), "y")
    ctx_step = next(ctx_ring)
    *step, product = tie(*step, product)
    step = ring.send(step)
    ctx_step = ctx_ring.send(ctx_step)
    other_product = swap(product[piece:], "core")
    *ctx_step, other_product = tie(*ctx_step, other_product)
    branch = ring.send(step).astype(BF16)
    branch = branch.reshape(1, group, own_count, features)
    branch = jnp.concatenate([branch, branch], 0).reshape(2 * group, own_count, features)
    branch = lax.all_to_all(branch, ("section", "y", "xh"), 0, 0, tiled=True)

    summed = ctx_ring.send(ctx_step)
    other_ctx = swap(summed[:, width:].astype(BF16), "xh")
    branch, other_ctx = tie(branch, other_ctx)
    ctx_grad = add(summed[:, :width], other_ctx)
    forward, received = local(
        functools.partial(finish_kernel, sizes),
        at,
        [branch.reshape(2, group, own_count, features), residual, early],
        [residual.shape, residual.shape],
    )

    own_rows = add(product[:piece], other_product)
    kept = own_rows[:, :width]
    came = swap(own_rows[:, width:], "xh")
    first = xh == 0
    weight_grad = jnp.concatenate([jnp.where(first, kept, came), jnp.where(first, came, kept)], 0)
    return (forward[None], received[None], ctx_grad[None], weight_grad[None])


def solution(mesh):
    fine = Mesh(mesh.devices.reshape(2, 4, 2, 8, 2), ("section", "y", "core", "z", "xh"))
    tokens = P("section", ("y", "core", "z", "xh"), None)
    heads = P("section", ("y", "core"), ("z", "xh"))
    return jax.shard_map(
        shards,
        mesh=fine,
        in_specs=(tokens, heads, P("section", None, ("z", "xh")), tokens),
        out_specs=(tokens, tokens, heads, heads),
        check_vma=False,
    )
```

```python
import functools
import math

import jax
import jax.numpy as jnp
from jax import lax
from jax.experimental import pallas as pl
from jax.experimental.pallas import tpu as pltpu
from jax.sharding import Mesh
from jax.sharding import PartitionSpec as P

BF16 = jnp.bfloat16
F32 = jnp.float32


def shift(value, axis, by):
    n = lax.axis_size(axis)
    return lax.ppermute(value, axis, [(i, (i + by) % n) for i in range(n)])


def swap(value, axis):
    return shift(value, axis, 1)


def add(a, b):
    return (a.astype(F32) + b.astype(F32)).astype(BF16)


def wrap(index, n):
    return index & (n - 1)


def pick(stack, index, axis=0):
    return lax.dynamic_index_in_dim(stack, index, axis, keepdims=False)


def place(buffer, block, starts):
    return lax.dynamic_update_slice(buffer, block, starts)


def tie(*values):
    return lax.optimization_barrier(values)


def both_ways(right, left, axis):
    return shift(right, axis, 1), shift(left, axis, -1)


def ring_gather(block, axis):
    far = lax.axis_size(axis) // 2
    half = block.shape[0] // 2
    blocks = {0: block}
    right = left = block
    for away in range(1, far):
        right, left = both_ways(right, left, axis)
        blocks[-away], blocks[away] = right, left
    return blocks, both_ways(right[:half], left[half:], axis)


def ring_steps(chunk, axis):
    far = lax.axis_size(axis) // 2
    opposite = chunk(far)
    half = opposite.shape[1] // 2
    low, high = yield both_ways(opposite[:, :half], opposite[:, half:], axis)
    ahead, behind = chunk(far - 1), chunk(1 - far)
    right = jnp.concatenate([add(ahead[:, :half], low), ahead[:, half:]], 1)
    left = jnp.concatenate([behind[:, :half], add(behind[:, half:], high)], 1)
    for away in range(far - 2, 0, -1):
        right, left = yield both_ways(right, left, axis)
        right, left = add(chunk(away), right), add(chunk(-away), left)
    right, left = yield both_ways(right, left, axis)
    yield chunk(0).astype(F32) + right.astype(F32) + left.astype(F32)


def by_group(n_y, n_core, n_xh, piece):
    for y in range(n_y):
        for xh in range(n_xh):
            for core in range(n_core):
                yield y * n_xh + xh, core, ((y * n_core + core) * n_xh + xh) * piece


def spread_kernel(sizes, at_ref, rows_ref, out_ref):
    piece = sizes[-1]
    core = at_ref[1]
    pieces = {(group, at): rows_ref[:, first : first + piece] for group, at, first in by_group(*sizes)}
    for group, at in pieces:
        chosen = jnp.where(core == 0, pieces[group, at], pieces[group, 1 - at])
        out_ref[group, :, at * piece : (at + 1) * piece] = chosen


def finish_kernel(sizes, at_ref, branch_ref, residual_ref, early_ref, forward_ref, received_ref):
    piece = sizes[-1]
    section, core = at_ref[0], at_ref[1]
    for group, at, first in by_group(*sizes):
        here = slice(first, first + piece)

        def term(of_section):
            mine, other = branch_ref[of_section, group, :, :piece], branch_ref[of_section, group, :, piece:]
            return jnp.where(core == at, mine, other).astype(F32)

        one, two = term(0), term(1)
        forward_ref[:, here] = (residual_ref[:, here].astype(F32) + jnp.where(section == 0, one, two)).astype(BF16)
        early = early_ref[:, here]
        received_ref[:, here] = jnp.where(section == 0, early, (early.astype(F32) + one).astype(BF16))


def local(kernel, at, arrays, shapes):
    whole = pl.BlockSpec(memory_space=pltpu.VMEM)
    return pl.pallas_call(
        kernel,
        out_shape=[jax.ShapeDtypeStruct(shape, BF16) for shape in shapes],
        in_specs=[pl.BlockSpec(memory_space=pltpu.SMEM)] + [whole] * len(arrays),
        out_specs=[whole] * len(shapes),
        compiler_params=pltpu.CompilerParams(vmem_limit_bytes=24 * 2**20),
    )(at, *arrays)


def shards(segment_input, context, out_proj, grad_output):
    residual = segment_input[0]
    contexts = context[0]
    weights = out_proj[0]
    upstream = grad_output[0]
    section, y, core, z, xh = (lax.axis_index(name) for name in ("section", "y", "core", "z", "xh"))
    n_y, n_core, n_z, n_xh = (lax.axis_size(name) for name in ("y", "core", "z", "xh"))
    own_count, model = upstream.shape
    group_tokens, width = contexts.shape
    piece = model // (n_y * n_core * n_xh)
    group = n_y * n_xh
    features = n_core * piece
    tokens = group_tokens * n_y
    z_tokens = own_count * n_xh
    block_tokens = own_count * group

    both = jnp.concatenate([contexts, swap(contexts, "xh")], 1)
    def rows(core_at, xh_at):
        return lax.dynamic_slice_in_dim(weights, ((y * n_core + core_at) * n_xh + xh_at) * piece, piece, 0)

    both, partner_rows = tie(both, rows(core, 1 - xh))
    came_rows = swap(partner_rows, "xh")
    other_rows = swap(came_rows, "core")
    block = jnp.concatenate(
        [jnp.concatenate([rows(core, xh), came_rows], 1), jnp.concatenate([rows(1 - core, xh), other_rows], 1)], 0
    )

    ctx_all = jnp.zeros((n_z, n_y, z_tokens, 2 * width), BF16)
    ctx_blocks, across = ring_gather(both, "y")
    ctx_blocks[n_y // 2] = jnp.concatenate(across, 0)
    for away, part in ctx_blocks.items():
        ctx_all = place(ctx_all, part.reshape(n_z, 1, z_tokens, 2 * width), (0, wrap(y + away, n_y), 0, 0))
    ctx_flat = ctx_all.reshape(tokens, 2 * width)

    sizes = (n_y, n_core, n_xh, piece)
    at = jnp.stack([section, core]).astype(jnp.int32)
    (spread,) = local(functools.partial(spread_kernel, sizes), at, [upstream], [(group, own_count, features)])
    spread = lax.all_to_all(spread, ("y", "xh"), 0, 0, tiled=True).reshape(block_tokens, features)
    grad_all = jnp.zeros((n_z, block_tokens, features), BF16)
    grad_blocks, far_blocks = ring_gather(spread, "z")
    for away, part in grad_blocks.items():
        grad_all = place(grad_all, part[None], (wrap(z + away, n_z), 0, 0))

    partial_branch = lax.dot_general(
        ctx_flat, block, (((1,), (1,)), ((), ())), preferred_element_type=F32
    ).astype(BF16).reshape(n_z, block_tokens, features)
    ring = ring_steps(lambda away: pick(partial_branch, wrap(z + away, n_z)), "z")
    *step, outgoing = tie(*next(ring), jnp.where(section == 0, residual, upstream))
    early = swap(outgoing, "section")
    step = ring.send(step)
    far = jnp.concatenate(far_blocks, 0)[None]
    grad_flat = place(grad_all, far, (wrap(z + n_z // 2, n_z), 0, 0)).reshape(tokens, features)
    partial_ctx = jnp.dot(grad_flat, block, preferred_element_type=F32).astype(BF16)
    *step, partial_ctx = tie(*step, partial_ctx)
    step = ring.send(step)
    norm_factor = 1.0 / math.sqrt(tokens * n_core)
    product = lax.dot_general(grad_flat, ctx_flat, (((0,), (0,)), ((), ())), preferred_element_type=F32)
    product, partial_ctx = tie((norm_factor * product).astype(BF16), partial_ctx)
    partial_ctx = partial_ctx.reshape(n_z, n_y, z_tokens, 2 * width)
    ctx_ring = ring_steps(lambda away: pick(partial_ctx, wrap(y + away, n_y), 1).reshape(group_tokens, 2 * width), "y")
    ctx_step = next(ctx_ring)
    other_product = swap(product[piece:], "core")
    *step, other_product, early = tie(*step, other_product, early)
    step = ring.send(step)
    ctx_step = ctx_ring.send(ctx_step)
    own_rows = add(product[:piece], other_product)
    came = swap(own_rows[:, width:], "xh")
    *ctx_step, came = tie(*ctx_step, came)
    branch = ring.send(step).astype(BF16)
    branch = branch.reshape(1, group, own_count, features)
    branch = jnp.concatenate([branch, branch], 0).reshape(2 * group, own_count, features)
    branch = lax.all_to_all(branch, ("section", "y", "xh"), 0, 0, tiled=True)

    summed = ctx_ring.send(ctx_step)
    other_ctx = swap(summed[:, width:].astype(BF16), "xh")
    branch, other_ctx = tie(branch, other_ctx)
    ctx_grad = add(summed[:, :width], other_ctx)
    forward, received = local(
        functools.partial(finish_kernel, sizes),
        at,
        [branch.reshape(2, group, own_count, features), residual, early],
        [residual.shape, residual.shape],
    )

    kept = own_rows[:, :width]
    first = xh == 0
    weight_grad = jnp.concatenate([jnp.where(first, kept, came), jnp.where(first, came, kept)], 0)
    return (forward[None], received[None], ctx_grad[None], weight_grad[None])


def solution(mesh):
    fine = Mesh(mesh.devices.reshape(2, 4, 2, 8, 2), ("section", "y", "core", "z", "xh"))
    tokens = P("section", ("y", "core", "z", "xh"), None)
    heads = P("section", ("y", "core"), ("z", "xh"))
    return jax.shard_map(
        shards,
        mesh=fine,
        in_specs=(tokens, heads, P("section", None, ("z", "xh")), tokens),
        out_specs=(tokens, tokens, heads, heads),
        check_vma=False,
    )
```

```python
import functools
import math

import jax
import jax.numpy as jnp
from jax import lax
from jax.experimental import pallas as pl
from jax.experimental.pallas import tpu as pltpu
from jax.sharding import Mesh
from jax.sharding import PartitionSpec as P

BF16 = jnp.bfloat16
F32 = jnp.float32


def shift(value, axis, by):
    n = lax.axis_size(axis)
    return lax.ppermute(value, axis, [(i, (i + by) % n) for i in range(n)])


def swap(value, axis):
    return shift(value, axis, 1)


def add(a, b):
    return (a.astype(F32) + b.astype(F32)).astype(BF16)


def wrap(index, n):
    return index & (n - 1)


def pick(stack, index, axis=0):
    return lax.dynamic_index_in_dim(stack, index, axis, keepdims=False)


def place(buffer, block, starts):
    return lax.dynamic_update_slice(buffer, block, starts)


def tie(*values):
    return lax.optimization_barrier(values)


def both_ways(right, left, axis):
    return shift(right, axis, 1), shift(left, axis, -1)


def ring_gather(block, axis):
    far = lax.axis_size(axis) // 2
    half = block.shape[0] // 2
    blocks = {0: block}
    right = left = block
    for away in range(1, far):
        right, left = both_ways(right, left, axis)
        blocks[-away], blocks[away] = right, left
    return blocks, both_ways(right[:half], left[half:], axis)


def ring_steps(chunk, axis):
    far = lax.axis_size(axis) // 2
    opposite = chunk(far)
    half = opposite.shape[1] // 2
    low, high = yield both_ways(opposite[:, :half], opposite[:, half:], axis)
    ahead, behind = chunk(far - 1), chunk(1 - far)
    right = jnp.concatenate([add(ahead[:, :half], low), ahead[:, half:]], 1)
    left = jnp.concatenate([behind[:, :half], add(behind[:, half:], high)], 1)
    for away in range(far - 2, 0, -1):
        right, left = yield both_ways(right, left, axis)
        right, left = add(chunk(away), right), add(chunk(-away), left)
    right, left = yield both_ways(right, left, axis)
    yield chunk(0).astype(F32) + right.astype(F32) + left.astype(F32)


def by_group(n_y, n_core, n_xh, piece):
    for y in range(n_y):
        for xh in range(n_xh):
            for core in range(n_core):
                yield y * n_xh + xh, core, ((y * n_core + core) * n_xh + xh) * piece


def spread_kernel(sizes, at_ref, rows_ref, out_ref):
    piece = sizes[-1]
    core = at_ref[1]
    pieces = {(group, at): rows_ref[:, first : first + piece] for group, at, first in by_group(*sizes)}
    for group, at in pieces:
        chosen = jnp.where(core == 0, pieces[group, at], pieces[group, 1 - at])
        out_ref[group, :, at * piece : (at + 1) * piece] = chosen


def finish_kernel(sizes, at_ref, branch_ref, residual_ref, early_ref, forward_ref, received_ref):
    piece = sizes[-1]
    section, core = at_ref[0], at_ref[1]
    for group, at, first in by_group(*sizes):
        here = slice(first, first + piece)

        def term(of_section):
            mine, other = branch_ref[of_section, group, :, :piece], branch_ref[of_section, group, :, piece:]
            return jnp.where(core == at, mine, other).astype(F32)

        one, two = term(0), term(1)
        forward_ref[:, here] = (residual_ref[:, here].astype(F32) + jnp.where(section == 0, one, two)).astype(BF16)
        early = early_ref[:, here]
        received_ref[:, here] = jnp.where(section == 0, early, (early.astype(F32) + one).astype(BF16))


def local(kernel, at, arrays, shapes):
    whole = pl.BlockSpec(memory_space=pltpu.VMEM)
    return pl.pallas_call(
        kernel,
        out_shape=[jax.ShapeDtypeStruct(shape, BF16) for shape in shapes],
        in_specs=[pl.BlockSpec(memory_space=pltpu.SMEM)] + [whole] * len(arrays),
        out_specs=[whole] * len(shapes),
        compiler_params=pltpu.CompilerParams(vmem_limit_bytes=24 * 2**20),
    )(at, *arrays)


def shards(segment_input, context, out_proj, grad_output):
    residual = segment_input[0]
    contexts = context[0]
    weights = out_proj[0]
    upstream = grad_output[0]
    section, y, core, z, xh = (lax.axis_index(name) for name in ("section", "y", "core", "z", "xh"))
    n_y, n_core, n_z, n_xh = (lax.axis_size(name) for name in ("y", "core", "z", "xh"))
    own_count, model = upstream.shape
    group_tokens, width = contexts.shape
    piece = model // (n_y * n_core * n_xh)
    group = n_y * n_xh
    features = n_core * piece
    tokens = group_tokens * n_y
    z_tokens = own_count * n_xh
    block_tokens = own_count * group

    both = jnp.concatenate([contexts, swap(contexts, "xh")], 1)
    def rows(core_at, xh_at):
        return lax.dynamic_slice_in_dim(weights, ((y * n_core + core_at) * n_xh + xh_at) * piece, piece, 0)

    both, partner_rows = tie(both, rows(core, 1 - xh))
    came_rows = swap(partner_rows, "xh")
    other_rows = swap(came_rows, "core")
    block = jnp.concatenate(
        [jnp.concatenate([rows(core, xh), came_rows], 1), jnp.concatenate([rows(1 - core, xh), other_rows], 1)], 0
    )

    ctx_all = jnp.zeros((n_z, n_y, z_tokens, 2 * width), BF16)
    ctx_blocks, across = ring_gather(both, "y")
    ctx_blocks[n_y // 2] = jnp.concatenate(across, 0)
    for away, part in ctx_blocks.items():
        ctx_all = place(ctx_all, part.reshape(n_z, 1, z_tokens, 2 * width), (0, wrap(y + away, n_y), 0, 0))
    ctx_flat = ctx_all.reshape(tokens, 2 * width)

    sizes = (n_y, n_core, n_xh, piece)
    at = jnp.stack([section, core]).astype(jnp.int32)
    (spread,) = local(functools.partial(spread_kernel, sizes), at, [upstream], [(group, own_count, features)])
    spread = lax.all_to_all(spread, ("y", "xh"), 0, 0, tiled=True).reshape(block_tokens, features)
    grad_all = jnp.zeros((n_z, block_tokens, features), BF16)
    grad_blocks, far_blocks = ring_gather(spread, "z")
    for away, part in grad_blocks.items():
        grad_all = place(grad_all, part[None], (wrap(z + away, n_z), 0, 0))

    partial_branch = lax.dot_general(
        ctx_flat, block, (((1,), (1,)), ((), ())), preferred_element_type=F32
    ).astype(BF16).reshape(n_z, block_tokens, features)
    ring = ring_steps(lambda away: pick(partial_branch, wrap(z + away, n_z)), "z")
    *step, outgoing = tie(*next(ring), jnp.where(section == 0, residual, upstream))
    early = swap(outgoing, "section")
    step = ring.send(step)
    far = jnp.concatenate(far_blocks, 0)[None]
    grad_flat = place(grad_all, far, (wrap(z + n_z // 2, n_z), 0, 0)).reshape(tokens, features)
    partial_ctx = jnp.dot(grad_flat, block, preferred_element_type=F32).astype(BF16)
    *step, partial_ctx = tie(*step, partial_ctx)
    step = ring.send(step)
    norm_factor = 1.0 / math.sqrt(tokens * n_core)

    def for_features(features_of):
        product = lax.dot_general(grad_flat, features_of, (((0,), (0,)), ((), ())), preferred_element_type=F32)
        return (norm_factor * product).astype(BF16)

    own_product = for_features(ctx_flat[:, :width])
    partner_product = swap(for_features(ctx_flat[:, width:]), "xh")
    other_product = swap(own_product[piece:], "core")
    partial_ctx = partial_ctx.reshape(n_z, n_y, z_tokens, 2 * width)
    ctx_ring = ring_steps(lambda away: pick(partial_ctx, wrap(y + away, n_y), 1).reshape(group_tokens, 2 * width), "y")
    *step, ctx_low, ctx_high, other_product, early = tie(*step, *next(ctx_ring), other_product, early)
    step = ring.send(step)
    ctx_step = ctx_ring.send((ctx_low, ctx_high))
    *ctx_step, partner_product = tie(*ctx_step, partner_product)
    branch = ring.send(step).astype(BF16)
    branch = branch.reshape(1, group, own_count, features)
    branch = jnp.concatenate([branch, branch], 0).reshape(2 * group, own_count, features)
    branch = lax.all_to_all(branch, ("section", "y", "xh"), 0, 0, tiled=True)

    summed = ctx_ring.send(ctx_step)
    other_ctx = swap(summed[:, width:].astype(BF16), "xh")
    other_partner = swap(partner_product[piece:], "core")
    branch, other_ctx, other_partner = tie(branch, other_ctx, other_partner)
    ctx_grad = add(summed[:, :width], other_ctx)
    forward, received = local(
        functools.partial(finish_kernel, sizes),
        at,
        [branch.reshape(2, group, own_count, features), residual, early],
        [residual.shape, residual.shape],
    )

    kept = add(own_product[:piece], other_product)
    came = add(partner_product[:piece], other_partner)
    first = xh == 0
    weight_grad = jnp.concatenate([jnp.where(first, kept, came), jnp.where(first, came, kept)], 0)
    return (forward[None], received[None], ctx_grad[None], weight_grad[None])


def solution(mesh):
    fine = Mesh(mesh.devices.reshape(2, 4, 2, 8, 2), ("section", "y", "core", "z", "xh"))
    tokens = P("section", ("y", "core", "z", "xh"), None)
    heads = P("section", ("y", "core"), ("z", "xh"))
    return jax.shard_map(
        shards,
        mesh=fine,
        in_specs=(tokens, heads, P("section", None, ("z", "xh")), tokens),
        out_specs=(tokens, tokens, heads, heads),
        check_vma=False,
    )
```

```python
import functools
import math

import jax
import jax.numpy as jnp
from jax import lax
from jax.experimental import pallas as pl
from jax.experimental.pallas import tpu as pltpu
from jax.sharding import Mesh
from jax.sharding import PartitionSpec as P

BF16 = jnp.bfloat16
F32 = jnp.float32


def shift(value, axis, by):
    n = lax.axis_size(axis)
    return lax.ppermute(value, axis, [(i, (i + by) % n) for i in range(n)])


def swap(value, axis):
    return shift(value, axis, 1)


def add(a, b):
    return (a.astype(F32) + b.astype(F32)).astype(BF16)


def wrap(index, n):
    return index & (n - 1)


def pick(stack, index, axis=0):
    return lax.dynamic_index_in_dim(stack, index, axis, keepdims=False)


def place(buffer, block, starts):
    return lax.dynamic_update_slice(buffer, block, starts)


def tie(*values):
    return lax.optimization_barrier(values)


def both_ways(right, left, axis):
    return shift(right, axis, 1), shift(left, axis, -1)


def ring_gather(block, axis):
    far = lax.axis_size(axis) // 2
    half = block.shape[0] // 2
    blocks = {0: block}
    right = left = block
    for away in range(1, far):
        right, left = both_ways(right, left, axis)
        blocks[-away], blocks[away] = right, left
    return blocks, both_ways(right[:half], left[half:], axis)


def ring_steps(chunk, axis):
    far = lax.axis_size(axis) // 2
    opposite = chunk(far)
    half = opposite.shape[1] // 2
    low, high = yield both_ways(opposite[:, :half], opposite[:, half:], axis)
    ahead, behind = chunk(far - 1), chunk(1 - far)
    right = jnp.concatenate([add(ahead[:, :half], low), ahead[:, half:]], 1)
    left = jnp.concatenate([behind[:, :half], add(behind[:, half:], high)], 1)
    for away in range(far - 2, 0, -1):
        right, left = yield both_ways(right, left, axis)
        right, left = add(chunk(away), right), add(chunk(-away), left)
    right, left = yield both_ways(right, left, axis)
    yield chunk(0).astype(F32) + right.astype(F32) + left.astype(F32)


def by_group(n_y, n_core, n_xh, piece):
    for y in range(n_y):
        for xh in range(n_xh):
            for core in range(n_core):
                yield y * n_xh + xh, core, ((y * n_core + core) * n_xh + xh) * piece


def spread_kernel(sizes, at_ref, rows_ref, out_ref):
    piece = sizes[-1]
    core = at_ref[1]
    pieces = {(group, at): rows_ref[:, first : first + piece] for group, at, first in by_group(*sizes)}
    for group, at in pieces:
        chosen = jnp.where(core == 0, pieces[group, at], pieces[group, 1 - at])
        out_ref[group, :, at * piece : (at + 1) * piece] = chosen


def finish_kernel(sizes, at_ref, branch_ref, residual_ref, early_ref, forward_ref, received_ref):
    piece = sizes[-1]
    section, core = at_ref[0], at_ref[1]
    for group, at, first in by_group(*sizes):
        here = slice(first, first + piece)

        def term(of_section):
            mine, other = branch_ref[of_section, group, :, :piece], branch_ref[of_section, group, :, piece:]
            return jnp.where(core == at, mine, other).astype(F32)

        one, two = term(0), term(1)
        forward_ref[:, here] = (residual_ref[:, here].astype(F32) + jnp.where(section == 0, one, two)).astype(BF16)
        early = early_ref[:, here]
        received_ref[:, here] = jnp.where(section == 0, early, (early.astype(F32) + one).astype(BF16))


def local(kernel, at, arrays, shapes):
    whole = pl.BlockSpec(memory_space=pltpu.VMEM)
    return pl.pallas_call(
        kernel,
        out_shape=[jax.ShapeDtypeStruct(shape, BF16) for shape in shapes],
        in_specs=[pl.BlockSpec(memory_space=pltpu.SMEM)] + [whole] * len(arrays),
        out_specs=[whole] * len(shapes),
        compiler_params=pltpu.CompilerParams(vmem_limit_bytes=24 * 2**20),
    )(at, *arrays)


def shards(segment_input, context, out_proj, grad_output):
    residual = segment_input[0]
    contexts = context[0]
    weights = out_proj[0]
    upstream = grad_output[0]
    section, y, core, z, xh = (lax.axis_index(name) for name in ("section", "y", "core", "z", "xh"))
    n_y, n_core, n_z, n_xh = (lax.axis_size(name) for name in ("y", "core", "z", "xh"))
    own_count, model = upstream.shape
    group_tokens, width = contexts.shape
    piece = model // (n_y * n_core * n_xh)
    group = n_y * n_xh
    features = n_core * piece
    tokens = group_tokens * n_y
    z_tokens = own_count * n_xh
    block_tokens = own_count * group

    both = jnp.concatenate([contexts, swap(contexts, "xh")], 1)
    def rows(core_at, xh_at):
        return lax.dynamic_slice_in_dim(weights, ((y * n_core + core_at) * n_xh + xh_at) * piece, piece, 0)

    both, partner_rows = tie(both, rows(core, 1 - xh))
    came_rows = swap(partner_rows, "xh")
    other_rows = swap(came_rows, "core")
    outgoing, came_rows = tie(jnp.where(section == 0, residual, upstream), came_rows)
    early = swap(outgoing, "section")
    block = jnp.concatenate(
        [jnp.concatenate([rows(core, xh), came_rows], 1), jnp.concatenate([rows(1 - core, xh), other_rows], 1)], 0
    )

    ctx_all = jnp.zeros((n_z, n_y, z_tokens, 2 * width), BF16)
    ctx_blocks, across = ring_gather(both, "y")
    ctx_blocks[n_y // 2] = jnp.concatenate(across, 0)
    for away, part in ctx_blocks.items():
        ctx_all = place(ctx_all, part.reshape(n_z, 1, z_tokens, 2 * width), (0, wrap(y + away, n_y), 0, 0))
    ctx_flat = ctx_all.reshape(tokens, 2 * width)

    sizes = (n_y, n_core, n_xh, piece)
    at = jnp.stack([section, core]).astype(jnp.int32)
    (spread,) = local(functools.partial(spread_kernel, sizes), at, [upstream], [(group, own_count, features)])
    spread = lax.all_to_all(spread, ("y", "xh"), 0, 0, tiled=True).reshape(block_tokens, features)
    grad_all = jnp.zeros((n_z, block_tokens, features), BF16)
    grad_blocks, far_blocks = ring_gather(spread, "z")
    for away, part in grad_blocks.items():
        grad_all = place(grad_all, part[None], (wrap(z + away, n_z), 0, 0))

    partial_branch = lax.dot_general(
        ctx_flat, block, (((1,), (1,)), ((), ())), preferred_element_type=F32
    ).astype(BF16).reshape(n_z, block_tokens, features)
    ring = ring_steps(lambda away: pick(partial_branch, wrap(z + away, n_z)), "z")
    *step, early = tie(*next(ring), early)
    step = ring.send(step)
    far = jnp.concatenate(far_blocks, 0)[None]
    grad_flat = place(grad_all, far, (wrap(z + n_z // 2, n_z), 0, 0)).reshape(tokens, features)
    partial_ctx = jnp.dot(grad_flat, block, preferred_element_type=F32).astype(BF16)
    *step, partial_ctx = tie(*step, partial_ctx)
    step = ring.send(step)
    norm_factor = 1.0 / math.sqrt(tokens * n_core)

    def for_features(features_of):
        product = lax.dot_general(grad_flat, features_of, (((0,), (0,)), ((), ())), preferred_element_type=F32)
        return (norm_factor * product).astype(BF16)

    own_product = for_features(ctx_flat[:, :width])
    partner_product = lax.all_gather(for_features(ctx_flat[:, width:]), "xh")
    other_product = swap(own_product[piece:], "core")
    partial_ctx = partial_ctx.reshape(n_z, n_y, z_tokens, 2 * width)
    ctx_ring = ring_steps(lambda away: pick(partial_ctx, wrap(y + away, n_y), 1).reshape(group_tokens, 2 * width), "y")
    *step, ctx_low, ctx_high, other_product = tie(*step, *next(ctx_ring), other_product)
    step = ring.send(step)
    ctx_step = ctx_ring.send((ctx_low, ctx_high))
    *ctx_step, partner_product = tie(*ctx_step, partner_product)
    partner_product = pick(partner_product, 1 - xh)
    branch = ring.send(step).astype(BF16)
    branch = branch.reshape(1, group, own_count, features)
    branch = jnp.concatenate([branch, branch], 0).reshape(2 * group, own_count, features)
    branch = lax.all_to_all(branch, ("section", "y", "xh"), 0, 0, tiled=True)

    summed = ctx_ring.send(ctx_step)
    other_ctx = swap(summed[:, width:].astype(BF16), "xh")
    other_partner = swap(partner_product[piece:], "core")
    branch, other_ctx, other_partner = tie(branch, other_ctx, other_partner)
    ctx_grad = add(summed[:, :width], other_ctx)
    forward, received = local(
        functools.partial(finish_kernel, sizes),
        at,
        [branch.reshape(2, group, own_count, features), residual, early],
        [residual.shape, residual.shape],
    )

    kept = add(own_product[:piece], other_product)
    came = add(partner_product[:piece], other_partner)
    weight_grad = place(jnp.zeros((n_xh * piece, width), BF16), kept, (xh * piece, 0))
    weight_grad = place(weight_grad, came, ((1 - xh) * piece, 0))
    return (forward[None], received[None], ctx_grad[None], weight_grad[None])


def solution(mesh):
    fine = Mesh(mesh.devices.reshape(2, 4, 2, 8, 2), ("section", "y", "core", "z", "xh"))
    tokens = P("section", ("y", "core", "z", "xh"), None)
    heads = P("section", ("y", "core"), ("z", "xh"))
    return jax.shard_map(
        shards,
        mesh=fine,
        in_specs=(tokens, heads, P("section", None, ("z", "xh")), tokens),
        out_specs=(tokens, tokens, heads, heads),
        check_vma=False,
    )
```

```python
import functools
import math

import jax
import jax.numpy as jnp
from jax import lax
from jax.experimental import pallas as pl
from jax.experimental.pallas import tpu as pltpu
from jax.sharding import Mesh
from jax.sharding import PartitionSpec as P

BF16 = jnp.bfloat16
F32 = jnp.float32


def shift(value, axis, by):
    n = lax.axis_size(axis)
    return lax.ppermute(value, axis, [(i, (i + by) % n) for i in range(n)])


def swap(value, axis):
    return shift(value, axis, 1)


def add(a, b):
    return (a.astype(F32) + b.astype(F32)).astype(BF16)


def wrap(index, n):
    return index & (n - 1)


def pick(stack, index, axis=0):
    return lax.dynamic_index_in_dim(stack, index, axis, keepdims=False)


def place(buffer, block, starts):
    return lax.dynamic_update_slice(buffer, block, starts)


def tie(*values):
    return lax.optimization_barrier(values)


def both_ways(right, left, axis):
    return shift(right, axis, 1), shift(left, axis, -1)


def ring_gather(block, axis):
    far = lax.axis_size(axis) // 2
    half = block.shape[0] // 2
    blocks = {0: block}
    right = left = block
    for away in range(1, far):
        right, left = both_ways(right, left, axis)
        blocks[-away], blocks[away] = right, left
    return blocks, both_ways(right[:half], left[half:], axis)


def ring_steps(chunk, axis):
    far = lax.axis_size(axis) // 2
    opposite = chunk(far)
    half = opposite.shape[1] // 2
    low, high = yield both_ways(opposite[:, :half], opposite[:, half:], axis)
    ahead, behind = chunk(far - 1), chunk(1 - far)
    right = jnp.concatenate([add(ahead[:, :half], low), ahead[:, half:]], 1)
    left = jnp.concatenate([behind[:, :half], add(behind[:, half:], high)], 1)
    for away in range(far - 2, 0, -1):
        right, left = yield both_ways(right, left, axis)
        right, left = add(chunk(away), right), add(chunk(-away), left)
    right, left = yield both_ways(right, left, axis)
    yield chunk(0).astype(F32) + right.astype(F32) + left.astype(F32)


def by_group(n_y, n_core, n_xh, piece):
    for y in range(n_y):
        for xh in range(n_xh):
            for core in range(n_core):
                yield y * n_xh + xh, core, ((y * n_core + core) * n_xh + xh) * piece


def spread_kernel(sizes, at_ref, rows_ref, out_ref):
    piece = sizes[-1]
    core = at_ref[1]
    pieces = {(group, at): rows_ref[:, first : first + piece] for group, at, first in by_group(*sizes)}
    for group, at in pieces:
        chosen = jnp.where(core == 0, pieces[group, at], pieces[group, 1 - at])
        out_ref[group, :, at * piece : (at + 1) * piece] = chosen


def finish_kernel(sizes, at_ref, branch_ref, residual_ref, early_ref, forward_ref, received_ref):
    piece = sizes[-1]
    section, core = at_ref[0], at_ref[1]
    for group, at, first in by_group(*sizes):
        here = slice(first, first + piece)

        def term(of_section):
            mine, other = branch_ref[of_section, group, :, :piece], branch_ref[of_section, group, :, piece:]
            return jnp.where(core == at, mine, other).astype(F32)

        one, two = term(0), term(1)
        forward_ref[:, here] = (residual_ref[:, here].astype(F32) + jnp.where(section == 0, one, two)).astype(BF16)
        early = early_ref[:, here]
        received_ref[:, here] = jnp.where(section == 0, early, (early.astype(F32) + one).astype(BF16))


def local(kernel, at, arrays, shapes):
    whole = pl.BlockSpec(memory_space=pltpu.VMEM)
    return pl.pallas_call(
        kernel,
        out_shape=[jax.ShapeDtypeStruct(shape, BF16) for shape in shapes],
        in_specs=[pl.BlockSpec(memory_space=pltpu.SMEM)] + [whole] * len(arrays),
        out_specs=[whole] * len(shapes),
        compiler_params=pltpu.CompilerParams(vmem_limit_bytes=24 * 2**20),
    )(at, *arrays)


def shards(segment_input, context, out_proj, grad_output):
    residual = segment_input[0]
    contexts = context[0]
    weights = out_proj[0]
    upstream = grad_output[0]
    section, y, core, z, xh = (lax.axis_index(name) for name in ("section", "y", "core", "z", "xh"))
    n_y, n_core, n_z, n_xh = (lax.axis_size(name) for name in ("y", "core", "z", "xh"))
    own_count, model = upstream.shape
    group_tokens, width = contexts.shape
    piece = model // (n_y * n_core * n_xh)
    group = n_y * n_xh
    features = n_core * piece
    tokens = group_tokens * n_y
    z_tokens = own_count * n_xh
    block_tokens = own_count * group

    both = jnp.concatenate([contexts, swap(contexts, "xh")], 1)
    def rows(core_at, xh_at):
        return lax.dynamic_slice_in_dim(weights, ((y * n_core + core_at) * n_xh + xh_at) * piece, piece, 0)

    both, partner_rows = tie(both, rows(core, 1 - xh))
    came_rows = swap(partner_rows, "xh")
    other_rows = swap(came_rows, "core")
    block = jnp.concatenate(
        [jnp.concatenate([rows(core, xh), came_rows], 1), jnp.concatenate([rows(1 - core, xh), other_rows], 1)], 0
    )

    ctx_all = jnp.zeros((n_z, n_y, z_tokens, 2 * width), BF16)
    ctx_blocks, across = ring_gather(both, "y")
    ctx_blocks[n_y // 2] = jnp.concatenate(across, 0)
    for away, part in ctx_blocks.items():
        ctx_all = place(ctx_all, part.reshape(n_z, 1, z_tokens, 2 * width), (0, wrap(y + away, n_y), 0, 0))
    ctx_flat = ctx_all.reshape(tokens, 2 * width)

    sizes = (n_y, n_core, n_xh, piece)
    at = jnp.stack([section, core]).astype(jnp.int32)
    (spread,) = local(functools.partial(spread_kernel, sizes), at, [upstream], [(group, own_count, features)])
    spread = lax.all_to_all(spread, ("y", "xh"), 0, 0, tiled=True).reshape(block_tokens, features)
    grad_all = jnp.zeros((n_z, block_tokens, features), BF16)
    grad_blocks, far_blocks = ring_gather(spread, "z")
    for away, part in grad_blocks.items():
        grad_all = place(grad_all, part[None], (wrap(z + away, n_z), 0, 0))

    partial_branch = lax.dot_general(
        ctx_flat, block, (((1,), (1,)), ((), ())), preferred_element_type=F32
    ).astype(BF16).reshape(n_z, block_tokens, features)
    ring = ring_steps(lambda away: pick(partial_branch, wrap(z + away, n_z)), "z")
    *step, outgoing = tie(*next(ring), jnp.where(section == 0, residual, upstream))
    early = swap(outgoing, "section")
    step = ring.send(step)
    far = jnp.concatenate(far_blocks, 0)[None]
    grad_flat = place(grad_all, far, (wrap(z + n_z // 2, n_z), 0, 0)).reshape(tokens, features)
    partial_ctx = jnp.dot(grad_flat, block, preferred_element_type=F32).astype(BF16)
    *step, partial_ctx = tie(*step, partial_ctx)
    step = ring.send(step)
    norm_factor = 1.0 / math.sqrt(tokens * n_core)

    def for_features(features_of):
        product = lax.dot_general(grad_flat, features_of, (((0,), (0,)), ((), ())), preferred_element_type=F32)
        return (norm_factor * product).astype(BF16)

    partner_product = for_features(ctx_flat[:, width:])
    partner_rows = add(partner_product[:piece], swap(partner_product[piece:], "core"))
    own_product = for_features(ctx_flat[:, :width])
    partial_ctx = partial_ctx.reshape(n_z, n_y, z_tokens, 2 * width)
    ctx_ring = ring_steps(lambda away: pick(partial_ctx, wrap(y + away, n_y), 1).reshape(group_tokens, 2 * width), "y")
    half = piece // 2
    came_first = swap(partner_rows[:half], "xh")
    *step, ctx_low, ctx_high, came_first, partner_rows, own_product, early = tie(
        *step, *next(ctx_ring), came_first, partner_rows, own_product, early
    )
    step = ring.send(step)
    ctx_step = ctx_ring.send((ctx_low, ctx_high))
    came_last = swap(partner_rows[half:], "xh")
    other_product = swap(own_product[piece:], "core")
    *ctx_step, other_product = tie(*ctx_step, other_product)
    *step, came_last = tie(*step, came_last)
    branch = ring.send(step).astype(BF16)
    branch = branch.reshape(1, group, own_count, features)
    branch = jnp.concatenate([branch, branch], 0).reshape(2 * group, own_count, features)
    branch = lax.all_to_all(branch, ("section", "y", "xh"), 0, 0, tiled=True)

    summed = ctx_ring.send(ctx_step)
    other_ctx = swap(summed[:, width:].astype(BF16), "xh")
    branch, other_ctx = tie(branch, other_ctx)
    ctx_grad = add(summed[:, :width], other_ctx)
    forward, received = local(
        functools.partial(finish_kernel, sizes),
        at,
        [branch.reshape(2, group, own_count, features), residual, early],
        [residual.shape, residual.shape],
    )

    kept = add(own_product[:piece], other_product)
    weight_grad = place(jnp.zeros((n_xh * piece, width), BF16), kept, (xh * piece, 0))
    weight_grad = place(weight_grad, came_first, ((1 - xh) * piece, 0))
    weight_grad = place(weight_grad, came_last, ((1 - xh) * piece + half, 0))
    return (forward[None], received[None], ctx_grad[None], weight_grad[None])


def solution(mesh):
    fine = Mesh(mesh.devices.reshape(2, 4, 2, 8, 2), ("section", "y", "core", "z", "xh"))
    tokens = P("section", ("y", "core", "z", "xh"), None)
    heads = P("section", ("y", "core"), ("z", "xh"))
    return jax.shard_map(
        shards,
        mesh=fine,
        in_specs=(tokens, heads, P("section", None, ("z", "xh")), tokens),
        out_specs=(tokens, tokens, heads, heads),
        check_vma=False,
    )
```

```python
import functools
import math

import jax
import jax.numpy as jnp
from jax import lax
from jax.experimental import pallas as pl
from jax.experimental.pallas import tpu as pltpu
from jax.sharding import Mesh
from jax.sharding import PartitionSpec as P

BF16 = jnp.bfloat16
F32 = jnp.float32


def shift(value, axis, by):
    n = lax.axis_size(axis)
    return lax.ppermute(value, axis, [(i, (i + by) % n) for i in range(n)])


def swap(value, axis):
    return shift(value, axis, 1)


def add(a, b):
    return (a.astype(F32) + b.astype(F32)).astype(BF16)


def wrap(index, n):
    return index & (n - 1)


def pick(stack, index, axis=0):
    return lax.dynamic_index_in_dim(stack, index, axis, keepdims=False)


def place(buffer, block, starts):
    return lax.dynamic_update_slice(buffer, block, starts)


def tie(*values):
    return lax.optimization_barrier(values)


def both_ways(right, left, axis):
    return shift(right, axis, 1), shift(left, axis, -1)


def ring_gather(block, axis):
    far = lax.axis_size(axis) // 2
    half = block.shape[0] // 2
    blocks = {0: block}
    right = left = block
    for away in range(1, far):
        right, left = both_ways(right, left, axis)
        blocks[-away], blocks[away] = right, left
    return blocks, both_ways(right[:half], left[half:], axis)


def ring_steps(chunk, axis):
    far = lax.axis_size(axis) // 2
    opposite = chunk(far)
    half = opposite.shape[1] // 2
    low, high = yield both_ways(opposite[:, :half], opposite[:, half:], axis)
    ahead, behind = chunk(far - 1), chunk(1 - far)
    right = jnp.concatenate([add(ahead[:, :half], low), ahead[:, half:]], 1)
    left = jnp.concatenate([behind[:, :half], add(behind[:, half:], high)], 1)
    for away in range(far - 2, 0, -1):
        right, left = yield both_ways(right, left, axis)
        right, left = add(chunk(away), right), add(chunk(-away), left)
    right, left = yield both_ways(right, left, axis)
    yield chunk(0).astype(F32) + right.astype(F32) + left.astype(F32)


def by_group(n_y, n_core, n_xh, piece):
    for y in range(n_y):
        for xh in range(n_xh):
            for core in range(n_core):
                yield y * n_xh + xh, core, ((y * n_core + core) * n_xh + xh) * piece


def spread_kernel(sizes, at_ref, rows_ref, out_ref):
    piece = sizes[-1]
    core = at_ref[1]
    pieces = {(group, at): rows_ref[:, first : first + piece] for group, at, first in by_group(*sizes)}
    for group, at in pieces:
        chosen = jnp.where(core == 0, pieces[group, at], pieces[group, 1 - at])
        out_ref[group, :, at * piece : (at + 1) * piece] = chosen


def finish_kernel(
    sizes, at_ref, branch_ref, residual_ref, early_ref, summed_ref, other_ref, forward_ref, received_ref, ctx_ref
):
    ctx_ref[...] = (summed_ref[:, : ctx_ref.shape[1]] + other_ref[...].astype(F32)).astype(BF16)
    piece = sizes[-1]
    section, core = at_ref[0], at_ref[1]
    for group, at, first in by_group(*sizes):
        here = slice(first, first + piece)

        def term(of_section):
            mine, other = branch_ref[of_section, group, :, :piece], branch_ref[of_section, group, :, piece:]
            return jnp.where(core == at, mine, other).astype(F32)

        one, two = term(0), term(1)
        forward_ref[:, here] = (residual_ref[:, here].astype(F32) + jnp.where(section == 0, one, two)).astype(BF16)
        early = early_ref[:, here]
        received_ref[:, here] = jnp.where(section == 0, early, (early.astype(F32) + one).astype(BF16))


def local(kernel, at, arrays, shapes):
    whole = pl.BlockSpec(memory_space=pltpu.VMEM)
    return pl.pallas_call(
        kernel,
        out_shape=[jax.ShapeDtypeStruct(shape, BF16) for shape in shapes],
        in_specs=[pl.BlockSpec(memory_space=pltpu.SMEM)] + [whole] * len(arrays),
        out_specs=[whole] * len(shapes),
        compiler_params=pltpu.CompilerParams(vmem_limit_bytes=24 * 2**20),
    )(at, *arrays)


def shards(segment_input, context, out_proj, grad_output):
    residual = segment_input[0]
    contexts = context[0]
    weights = out_proj[0]
    upstream = grad_output[0]
    section, y, core, z, xh = (lax.axis_index(name) for name in ("section", "y", "core", "z", "xh"))
    n_y, n_core, n_z, n_xh = (lax.axis_size(name) for name in ("y", "core", "z", "xh"))
    own_count, model = upstream.shape
    group_tokens, width = contexts.shape
    piece = model // (n_y * n_core * n_xh)
    group = n_y * n_xh
    features = n_core * piece
    tokens = group_tokens * n_y
    z_tokens = own_count * n_xh
    block_tokens = own_count * group

    both = jnp.concatenate([contexts, swap(contexts, "xh")], 1)
    def rows(core_at, xh_at):
        return lax.dynamic_slice_in_dim(weights, ((y * n_core + core_at) * n_xh + xh_at) * piece, piece, 0)

    both, partner_rows = tie(both, rows(core, 1 - xh))
    came_rows = swap(partner_rows, "xh")
    other_rows = swap(came_rows, "core")
    block = jnp.concatenate(
        [jnp.concatenate([rows(core, xh), came_rows], 1), jnp.concatenate([rows(1 - core, xh), other_rows], 1)], 0
    )

    ctx_all = jnp.zeros((n_z, n_y, z_tokens, 2 * width), BF16)
    ctx_blocks, across = ring_gather(both, "y")
    ctx_blocks[n_y // 2] = jnp.concatenate(across, 0)
    for away, part in ctx_blocks.items():
        ctx_all = place(ctx_all, part.reshape(n_z, 1, z_tokens, 2 * width), (0, wrap(y + away, n_y), 0, 0))
    ctx_flat = ctx_all.reshape(tokens, 2 * width)

    sizes = (n_y, n_core, n_xh, piece)
    at = jnp.stack([section, core]).astype(jnp.int32)
    (spread,) = local(functools.partial(spread_kernel, sizes), at, [upstream], [(group, own_count, features)])
    spread = lax.all_to_all(spread, ("y", "xh"), 0, 0, tiled=True).reshape(block_tokens, features)
    grad_all = jnp.zeros((n_z, block_tokens, features), BF16)
    grad_blocks, far_blocks = ring_gather(spread, "z")
    for away, part in grad_blocks.items():
        grad_all = place(grad_all, part[None], (wrap(z + away, n_z), 0, 0))

    partial_branch = lax.dot_general(
        ctx_flat, block, (((1,), (1,)), ((), ())), preferred_element_type=F32
    ).astype(BF16).reshape(n_z, block_tokens, features)
    ring = ring_steps(lambda away: pick(partial_branch, wrap(z + away, n_z)), "z")
    *step, outgoing = tie(*next(ring), jnp.where(section == 0, residual, upstream))
    early = swap(outgoing, "section")
    step = ring.send(step)
    far = jnp.concatenate(far_blocks, 0)[None]
    grad_flat = place(grad_all, far, (wrap(z + n_z // 2, n_z), 0, 0)).reshape(tokens, features)
    partial_ctx = jnp.dot(grad_flat, block, preferred_element_type=F32).astype(BF16)
    *step, partial_ctx, early = tie(*step, partial_ctx, early)
    step = ring.send(step)
    norm_factor = 1.0 / math.sqrt(tokens * n_core)
    product = lax.dot_general(grad_flat, ctx_flat, (((0,), (0,)), ((), ())), preferred_element_type=F32)
    product, partial_ctx = tie((norm_factor * product).astype(BF16), partial_ctx)
    partial_ctx = partial_ctx.reshape(n_z, n_y, z_tokens, 2 * width)
    ctx_ring = ring_steps(lambda away: pick(partial_ctx, wrap(y + away, n_y), 1).reshape(group_tokens, 2 * width), "y")
    ctx_step = next(ctx_ring)
    other_product = swap(product[piece:], "core")
    *step, ctx_low, ctx_high, other_product = tie(*step, *ctx_step, other_product)
    step = ring.send(step)
    ctx_step = ctx_ring.send((ctx_low, ctx_high))
    own_rows = add(product[:piece], other_product)
    came = swap(own_rows[:, width:], "xh")
    *ctx_step, came = tie(*ctx_step, came)
    branch = ring.send(step).astype(BF16)
    branch = branch.reshape(1, group, own_count, features)
    branch = jnp.concatenate([branch, branch], 0).reshape(2 * group, own_count, features)
    branch = lax.all_to_all(branch, ("section", "y", "xh"), 0, 0, tiled=True)

    summed = ctx_ring.send(ctx_step)
    other_ctx = swap(summed[:, width:].astype(BF16), "xh")
    forward, received, ctx_grad = local(
        functools.partial(finish_kernel, sizes),
        at,
        [branch.reshape(2, group, own_count, features), residual, early, summed, other_ctx],
        [residual.shape, residual.shape, other_ctx.shape],
    )

    weight_grad = place(jnp.zeros((n_xh * piece, width), BF16), own_rows[:, :width], (xh * piece, 0))
    weight_grad = place(weight_grad, came, ((1 - xh) * piece, 0))
    return (forward[None], received[None], ctx_grad[None], weight_grad[None])


def solution(mesh):
    fine = Mesh(mesh.devices.reshape(2, 4, 2, 8, 2), ("section", "y", "core", "z", "xh"))
    tokens = P("section", ("y", "core", "z", "xh"), None)
    heads = P("section", ("y", "core"), ("z", "xh"))
    return jax.shard_map(
        shards,
        mesh=fine,
        in_specs=(tokens, heads, P("section", None, ("z", "xh")), tokens),
        out_specs=(tokens, tokens, heads, heads),
        check_vma=False,
    )
```

```python
import functools
import math

import jax
import jax.numpy as jnp
from jax import lax
from jax.experimental import pallas as pl
from jax.experimental.pallas import tpu as pltpu
from jax.sharding import Mesh
from jax.sharding import PartitionSpec as P

BF16 = jnp.bfloat16
F32 = jnp.float32


def shift(value, axis, by):
    n = lax.axis_size(axis)
    return lax.ppermute(value, axis, [(i, (i + by) % n) for i in range(n)])


def swap(value, axis):
    return shift(value, axis, 1)


def add(a, b):
    return (a.astype(F32) + b.astype(F32)).astype(BF16)


def wrap(index, n):
    return index & (n - 1)


def pick(stack, index, axis=0):
    return lax.dynamic_index_in_dim(stack, index, axis, keepdims=False)


def place(buffer, block, starts):
    return lax.dynamic_update_slice(buffer, block, starts)


def tie(*values):
    return lax.optimization_barrier(values)


def both_ways(right, left, axis):
    return shift(right, axis, 1), shift(left, axis, -1)


def ring_gather(block, axis):
    far = lax.axis_size(axis) // 2
    half = block.shape[0] // 2
    blocks = {0: block}
    right = left = block
    for away in range(1, far):
        right, left = both_ways(right, left, axis)
        blocks[-away], blocks[away] = right, left
    return blocks, both_ways(right[:half], left[half:], axis)


def ring_steps(chunk, axis):
    far = lax.axis_size(axis) // 2
    opposite = chunk(far)
    half = opposite.shape[1] // 2
    low, high = yield both_ways(opposite[:, :half], opposite[:, half:], axis)
    ahead, behind = chunk(far - 1), chunk(1 - far)
    right = jnp.concatenate([add(ahead[:, :half], low), ahead[:, half:]], 1)
    left = jnp.concatenate([behind[:, :half], add(behind[:, half:], high)], 1)
    for away in range(far - 2, 0, -1):
        right, left = yield both_ways(right, left, axis)
        right, left = add(chunk(away), right), add(chunk(-away), left)
    right, left = yield both_ways(right, left, axis)
    yield chunk(0).astype(F32) + right.astype(F32) + left.astype(F32)


def by_group(n_y, n_core, n_xh, piece):
    for y in range(n_y):
        for xh in range(n_xh):
            for core in range(n_core):
                yield y * n_xh + xh, core, ((y * n_core + core) * n_xh + xh) * piece


def spread_kernel(sizes, at_ref, rows_ref, out_ref):
    piece = sizes[-1]
    core = at_ref[1]
    pieces = {(group, at): rows_ref[:, first : first + piece] for group, at, first in by_group(*sizes)}
    for group, at in pieces:
        chosen = jnp.where(core == 0, pieces[group, at], pieces[group, 1 - at])
        out_ref[group, :, at * piece : (at + 1) * piece] = chosen


def finish_kernel(
    sizes, at_ref, branch_ref, residual_ref, early_ref, summed_ref, other_ref, forward_ref, received_ref, ctx_ref
):
    ctx_ref[...] = (summed_ref[:, : ctx_ref.shape[1]] + other_ref[...].astype(F32)).astype(BF16)
    piece = sizes[-1]
    section, core = at_ref[0], at_ref[1]
    for group, at, first in by_group(*sizes):
        here = slice(first, first + piece)

        def term(of_section):
            mine, other = branch_ref[of_section, group, :, :piece], branch_ref[of_section, group, :, piece:]
            return jnp.where(core == at, mine, other).astype(F32)

        one, two = term(0), term(1)
        forward_ref[:, here] = (residual_ref[:, here].astype(F32) + jnp.where(section == 0, one, two)).astype(BF16)
        early = early_ref[:, here]
        received_ref[:, here] = jnp.where(section == 0, early, (early.astype(F32) + one).astype(BF16))


def local(kernel, at, arrays, shapes):
    whole = pl.BlockSpec(memory_space=pltpu.VMEM)
    return pl.pallas_call(
        kernel,
        out_shape=[jax.ShapeDtypeStruct(shape, BF16) for shape in shapes],
        in_specs=[pl.BlockSpec(memory_space=pltpu.SMEM)] + [whole] * len(arrays),
        out_specs=[whole] * len(shapes),
        compiler_params=pltpu.CompilerParams(vmem_limit_bytes=24 * 2**20),
    )(at, *arrays)


def shards(segment_input, context, out_proj, grad_output):
    residual = segment_input[0]
    contexts = context[0]
    weights = out_proj[0]
    upstream = grad_output[0]
    section, y, core, z, xh = (lax.axis_index(name) for name in ("section", "y", "core", "z", "xh"))
    n_y, n_core, n_z, n_xh = (lax.axis_size(name) for name in ("y", "core", "z", "xh"))
    own_count, model = upstream.shape
    group_tokens, width = contexts.shape
    piece = model // (n_y * n_core * n_xh)
    group = n_y * n_xh
    features = n_core * piece
    tokens = group_tokens * n_y
    z_tokens = own_count * n_xh
    block_tokens = own_count * group

    both = jnp.concatenate([contexts, swap(contexts, "xh")], 1)
    def rows(core_at, xh_at):
        return lax.dynamic_slice_in_dim(weights, ((y * n_core + core_at) * n_xh + xh_at) * piece, piece, 0)

    both, partner_rows = tie(both, rows(core, 1 - xh))
    came_rows = swap(partner_rows, "xh")
    other_rows = swap(came_rows, "core")
    block = jnp.concatenate(
        [jnp.concatenate([rows(core, xh), came_rows], 1), jnp.concatenate([rows(1 - core, xh), other_rows], 1)], 0
    )

    ctx_all = jnp.zeros((n_z, n_y, z_tokens, 2 * width), BF16)
    ctx_blocks, across = ring_gather(both, "y")
    ctx_blocks[n_y // 2] = jnp.concatenate(across, 0)
    for away, part in ctx_blocks.items():
        ctx_all = place(ctx_all, part.reshape(n_z, 1, z_tokens, 2 * width), (0, wrap(y + away, n_y), 0, 0))
    ctx_flat = ctx_all.reshape(tokens, 2 * width)

    sizes = (n_y, n_core, n_xh, piece)
    at = jnp.stack([section, core]).astype(jnp.int32)
    (spread,) = local(functools.partial(spread_kernel, sizes), at, [upstream], [(group, own_count, features)])
    spread = lax.all_to_all(spread, ("y", "xh"), 0, 0, tiled=True).reshape(block_tokens, features)
    grad_all = jnp.zeros((n_z, block_tokens, features), BF16)
    grad_blocks, far_blocks = ring_gather(spread, "z")
    for away, part in grad_blocks.items():
        grad_all = place(grad_all, part[None], (wrap(z + away, n_z), 0, 0))

    partial_branch = lax.dot_general(
        ctx_flat, block, (((1,), (1,)), ((), ())), preferred_element_type=F32
    ).astype(BF16).reshape(n_z, block_tokens, features)
    ring = ring_steps(lambda away: pick(partial_branch, wrap(z + away, n_z)), "z")
    *step, outgoing = tie(*next(ring), jnp.where(section == 0, residual, upstream))
    early = swap(outgoing, "section")
    step = ring.send(step)
    far = jnp.concatenate(far_blocks, 0)[None]
    grad_flat = place(grad_all, far, (wrap(z + n_z // 2, n_z), 0, 0)).reshape(tokens, features)
    partial_ctx = jnp.dot(grad_flat, block, preferred_element_type=F32).astype(BF16)
    *step, partial_ctx = tie(*step, partial_ctx)
    step = ring.send(step)
    norm_factor = 1.0 / math.sqrt(tokens * n_core)
    product = lax.dot_general(grad_flat, ctx_flat, (((0,), (0,)), ((), ())), preferred_element_type=F32)
    product, partial_ctx = tie((norm_factor * product).astype(BF16), partial_ctx)
    partial_ctx = partial_ctx.reshape(n_z, n_y, z_tokens, 2 * width)
    ctx_ring = ring_steps(lambda away: pick(partial_ctx, wrap(y + away, n_y), 1).reshape(group_tokens, 2 * width), "y")
    ctx_step = next(ctx_ring)
    other_product = swap(product[piece:], "core")
    *step, other_product, early = tie(*step, other_product, early)
    step = ring.send(step)
    ctx_step = ctx_ring.send(ctx_step)
    own_rows = add(product[:piece], other_product)
    half = piece // 2
    came_first = swap(own_rows[:half, width:], "xh")
    *ctx_step, came_first = tie(*ctx_step, came_first)
    came_last = swap(own_rows[half:, width:], "xh")
    branch = ring.send(step).astype(BF16)
    branch = branch.reshape(1, group, own_count, features)
    branch = jnp.concatenate([branch, branch], 0).reshape(2 * group, own_count, features)
    branch = lax.all_to_all(branch, ("section", "y", "xh"), 0, 0, tiled=True)

    summed = ctx_ring.send(ctx_step)
    other_ctx = swap(summed[:, width:].astype(BF16), "xh")
    branch, other_ctx, came_last = tie(branch, other_ctx, came_last)
    forward, received, ctx_grad = local(
        functools.partial(finish_kernel, sizes),
        at,
        [branch.reshape(2, group, own_count, features), residual, early, summed, other_ctx],
        [residual.shape, residual.shape, other_ctx.shape],
    )

    weight_grad = place(jnp.zeros((n_xh * piece, width), BF16), own_rows[:, :width], (xh * piece, 0))
    weight_grad = place(weight_grad, came_first, ((1 - xh) * piece, 0))
    weight_grad = place(weight_grad, came_last, ((1 - xh) * piece + half, 0))
    return (forward[None], received[None], ctx_grad[None], weight_grad[None])


def solution(mesh):
    fine = Mesh(mesh.devices.reshape(2, 4, 2, 8, 2), ("section", "y", "core", "z", "xh"))
    tokens = P("section", ("y", "core", "z", "xh"), None)
    heads = P("section", ("y", "core"), ("z", "xh"))
    return jax.shard_map(
        shards,
        mesh=fine,
        in_specs=(tokens, heads, P("section", None, ("z", "xh")), tokens),
        out_specs=(tokens, tokens, heads, heads),
        check_vma=False,
    )
```

```python
import functools
import math

import jax
import jax.numpy as jnp
from jax import lax
from jax.experimental import pallas as pl
from jax.experimental.pallas import tpu as pltpu
from jax.sharding import Mesh
from jax.sharding import PartitionSpec as P

BF16 = jnp.bfloat16
F32 = jnp.float32


def shift(value, axis, by):
    n = lax.axis_size(axis)
    return lax.ppermute(value, axis, [(i, (i + by) % n) for i in range(n)])


def swap(value, axis):
    return shift(value, axis, 1)


def add(a, b):
    return (a.astype(F32) + b.astype(F32)).astype(BF16)


def wrap(index, n):
    return index & (n - 1)


def pick(stack, index, axis=0):
    return lax.dynamic_index_in_dim(stack, index, axis, keepdims=False)


def place(buffer, block, starts):
    return lax.dynamic_update_slice(buffer, block, starts)


def tie(*values):
    return lax.optimization_barrier(values)


def both_ways(right, left, axis):
    return shift(right, axis, 1), shift(left, axis, -1)


def ring_gather(block, axis):
    far = lax.axis_size(axis) // 2
    half = block.shape[0] // 2
    blocks = {0: block}
    right = left = block
    for away in range(1, far):
        right, left = both_ways(right, left, axis)
        blocks[-away], blocks[away] = right, left
    return blocks, both_ways(right[:half], left[half:], axis)


def ring_steps(chunk, axis):
    far = lax.axis_size(axis) // 2
    opposite = chunk(far)
    half = opposite.shape[1] // 2
    low, high = yield both_ways(opposite[:, :half], opposite[:, half:], axis)
    ahead, behind = chunk(far - 1), chunk(1 - far)
    right = jnp.concatenate([add(ahead[:, :half], low), ahead[:, half:]], 1)
    left = jnp.concatenate([behind[:, :half], add(behind[:, half:], high)], 1)
    for away in range(far - 2, 0, -1):
        right, left = yield both_ways(right, left, axis)
        right, left = add(chunk(away), right), add(chunk(-away), left)
    right, left = yield both_ways(right, left, axis)
    yield chunk(0).astype(F32) + right.astype(F32) + left.astype(F32)


def by_group(n_y, n_core, n_xh, piece):
    for y in range(n_y):
        for xh in range(n_xh):
            for core in range(n_core):
                yield y * n_xh + xh, core, ((y * n_core + core) * n_xh + xh) * piece


def spread_kernel(sizes, at_ref, rows_ref, out_ref):
    piece = sizes[-1]
    core = at_ref[1]
    pieces = {(group, at): rows_ref[:, first : first + piece] for group, at, first in by_group(*sizes)}
    for group, at in pieces:
        chosen = jnp.where(core == 0, pieces[group, at], pieces[group, 1 - at])
        out_ref[group, :, at * piece : (at + 1) * piece] = chosen


def finish_kernel(
    sizes, at_ref, branch_ref, residual_ref, early_ref, summed_ref, other_ref, forward_ref, received_ref, ctx_ref
):
    ctx_ref[...] = (summed_ref[:, : ctx_ref.shape[1]] + other_ref[...].astype(F32)).astype(BF16)
    piece = sizes[-1]
    section, core = at_ref[0], at_ref[1]
    for group, at, first in by_group(*sizes):
        here = slice(first, first + piece)

        def term(of_section):
            mine, other = branch_ref[of_section, group, :, :piece], branch_ref[of_section, group, :, piece:]
            return jnp.where(core == at, mine, other).astype(F32)

        one, two = term(0), term(1)
        forward_ref[:, here] = (residual_ref[:, here].astype(F32) + jnp.where(section == 0, one, two)).astype(BF16)
        early = early_ref[:, here]
        received_ref[:, here] = jnp.where(section == 0, early, (early.astype(F32) + one).astype(BF16))


def local(kernel, at, arrays, shapes):
    whole = pl.BlockSpec(memory_space=pltpu.VMEM)
    return pl.pallas_call(
        kernel,
        out_shape=[jax.ShapeDtypeStruct(shape, BF16) for shape in shapes],
        in_specs=[pl.BlockSpec(memory_space=pltpu.SMEM)] + [whole] * len(arrays),
        out_specs=[whole] * len(shapes),
        compiler_params=pltpu.CompilerParams(vmem_limit_bytes=24 * 2**20),
    )(at, *arrays)


def shards(segment_input, context, out_proj, grad_output):
    residual = segment_input[0]
    contexts = context[0]
    weights = out_proj[0]
    upstream = grad_output[0]
    section, y, core, z, xh = (lax.axis_index(name) for name in ("section", "y", "core", "z", "xh"))
    n_y, n_core, n_z, n_xh = (lax.axis_size(name) for name in ("y", "core", "z", "xh"))
    own_count, model = upstream.shape
    group_tokens, width = contexts.shape
    piece = model // (n_y * n_core * n_xh)
    group = n_y * n_xh
    features = n_core * piece
    tokens = group_tokens * n_y
    z_tokens = own_count * n_xh
    block_tokens = own_count * group

    both = jnp.concatenate([contexts, swap(contexts, "xh")], 1)
    def rows(core_at, xh_at):
        return lax.dynamic_slice_in_dim(weights, ((y * n_core + core_at) * n_xh + xh_at) * piece, piece, 0)

    both, partner_rows = tie(both, rows(core, 1 - xh))
    came_rows = swap(partner_rows, "xh")
    other_rows = swap(came_rows, "core")
    block = jnp.concatenate(
        [jnp.concatenate([rows(core, xh), came_rows], 1), jnp.concatenate([rows(1 - core, xh), other_rows], 1)], 0
    )

    ctx_all = jnp.zeros((n_z, n_y, z_tokens, 2 * width), BF16)
    ctx_blocks, across = ring_gather(both, "y")
    ctx_blocks[n_y // 2] = jnp.concatenate(across, 0)
    for away, part in ctx_blocks.items():
        ctx_all = place(ctx_all, part.reshape(n_z, 1, z_tokens, 2 * width), (0, wrap(y + away, n_y), 0, 0))
    ctx_flat = ctx_all.reshape(tokens, 2 * width)

    sizes = (n_y, n_core, n_xh, piece)
    at = jnp.stack([section, core]).astype(jnp.int32)
    (spread,) = local(functools.partial(spread_kernel, sizes), at, [upstream], [(group, own_count, features)])
    spread = lax.all_to_all(spread, ("y", "xh"), 0, 0, tiled=True).reshape(block_tokens, features)
    grad_all = jnp.zeros((n_z, block_tokens, features), BF16)
    grad_blocks, far_blocks = ring_gather(spread, "z")
    for away, part in grad_blocks.items():
        grad_all = place(grad_all, part[None], (wrap(z + away, n_z), 0, 0))

    partial_branch = lax.dot_general(
        ctx_flat, block, (((1,), (1,)), ((), ())), preferred_element_type=F32
    ).astype(BF16).reshape(n_z, block_tokens, features)
    ring = ring_steps(lambda away: pick(partial_branch, wrap(z + away, n_z)), "z")
    *step, outgoing = tie(*next(ring), jnp.where(section == 0, residual, upstream))
    early = swap(outgoing, "section")
    step = ring.send(step)
    far = jnp.concatenate(far_blocks, 0)[None]
    grad_flat = place(grad_all, far, (wrap(z + n_z // 2, n_z), 0, 0)).reshape(tokens, features)
    partial_ctx = jnp.dot(grad_flat, block, preferred_element_type=F32).astype(BF16)
    *step, partial_ctx = tie(*step, partial_ctx)
    step = ring.send(step)
    norm_factor = 1.0 / math.sqrt(tokens * n_core)
    product = lax.dot_general(grad_flat, ctx_flat, (((0,), (0,)), ((), ())), preferred_element_type=F32)
    product, partial_ctx = tie((norm_factor * product).astype(BF16), partial_ctx)
    partial_ctx = partial_ctx.reshape(n_z, n_y, z_tokens, 2 * width)
    ctx_ring = ring_steps(lambda away: pick(partial_ctx, wrap(y + away, n_y), 1).reshape(group_tokens, 2 * width), "y")
    ctx_step = next(ctx_ring)
    other_product = swap(product[piece:], "core")
    *step, other_product, early = tie(*step, other_product, early)
    step = ring.send(step)
    ctx_step = ctx_ring.send(ctx_step)
    own_rows = add(product[:piece], other_product)
    half = piece // 2
    came_first = swap(own_rows[:half, width:], "xh")
    *ctx_step, came_first = tie(*ctx_step, came_first)
    came_last = swap(own_rows[half:, width:], "xh")
    branch = ring.send(step).astype(BF16)
    branch = branch.reshape(1, group, own_count, features)
    branch = jnp.concatenate([branch, branch], 0).reshape(2 * group, own_count, features)
    branch = lax.all_to_all(branch, ("section", "y", "xh"), 0, 0, tiled=True)

    summed = ctx_ring.send(ctx_step)
    other_ctx = swap(summed[:, width:].astype(BF16), "xh")
    branch, other_ctx = tie(branch, other_ctx)
    forward, received, ctx_grad = local(
        functools.partial(finish_kernel, sizes),
        at,
        [branch.reshape(2, group, own_count, features), residual, early, summed, other_ctx],
        [residual.shape, residual.shape, other_ctx.shape],
    )

    weight_grad = place(jnp.zeros((n_xh * piece, width), BF16), own_rows[:, :width], (xh * piece, 0))
    weight_grad = place(weight_grad, came_first, ((1 - xh) * piece, 0))
    weight_grad = place(weight_grad, came_last, ((1 - xh) * piece + half, 0))
    return (forward[None], received[None], ctx_grad[None], weight_grad[None])


def solution(mesh):
    fine = Mesh(mesh.devices.reshape(2, 4, 2, 8, 2), ("section", "y", "core", "z", "xh"))
    tokens = P("section", ("y", "core", "z", "xh"), None)
    heads = P("section", ("y", "core"), ("z", "xh"))
    return jax.shard_map(
        shards,
        mesh=fine,
        in_specs=(tokens, heads, P("section", None, ("z", "xh")), tokens),
        out_specs=(tokens, tokens, heads, heads),
        check_vma=False,
    )
```

```python
import functools
import math

import jax
import jax.numpy as jnp
from jax import lax
from jax.experimental import pallas as pl
from jax.experimental.pallas import tpu as pltpu
from jax.sharding import Mesh
from jax.sharding import PartitionSpec as P

BF16 = jnp.bfloat16
F32 = jnp.float32


def shift(value, axis, by):
    n = lax.axis_size(axis)
    return lax.ppermute(value, axis, [(i, (i + by) % n) for i in range(n)])


def swap(value, axis):
    return shift(value, axis, 1)


def add(a, b):
    return (a.astype(F32) + b.astype(F32)).astype(BF16)


def wrap(index, n):
    return index & (n - 1)


def pick(stack, index, axis=0):
    return lax.dynamic_index_in_dim(stack, index, axis, keepdims=False)


def place(buffer, block, starts):
    return lax.dynamic_update_slice(buffer, block, starts)


def tie(*values):
    return lax.optimization_barrier(values)


def both_ways(right, left, axis):
    return shift(right, axis, 1), shift(left, axis, -1)


def ring_gather(block, axis):
    far = lax.axis_size(axis) // 2
    half = block.shape[0] // 2
    blocks = {0: block}
    right = left = block
    for away in range(1, far):
        right, left = both_ways(right, left, axis)
        blocks[-away], blocks[away] = right, left
    return blocks, both_ways(right[:half], left[half:], axis)


def ring_steps(chunk, axis):
    far = lax.axis_size(axis) // 2
    opposite = chunk(far)
    half = opposite.shape[1] // 2
    low, high = yield both_ways(opposite[:, :half], opposite[:, half:], axis)
    ahead, behind = chunk(far - 1), chunk(1 - far)
    right = jnp.concatenate([add(ahead[:, :half], low), ahead[:, half:]], 1)
    left = jnp.concatenate([behind[:, :half], add(behind[:, half:], high)], 1)
    for away in range(far - 2, 0, -1):
        right, left = yield both_ways(right, left, axis)
        right, left = add(chunk(away), right), add(chunk(-away), left)
    right, left = yield both_ways(right, left, axis)
    yield chunk(0).astype(F32) + right.astype(F32) + left.astype(F32)


def by_group(n_y, n_core, n_xh, piece):
    for y in range(n_y):
        for xh in range(n_xh):
            for core in range(n_core):
                yield y * n_xh + xh, core, ((y * n_core + core) * n_xh + xh) * piece


def spread_kernel(sizes, at_ref, rows_ref, out_ref):
    piece = sizes[-1]
    core = at_ref[1]
    pieces = {(group, at): rows_ref[:, first : first + piece] for group, at, first in by_group(*sizes)}
    for group, at in pieces:
        chosen = jnp.where(core == 0, pieces[group, at], pieces[group, 1 - at])
        out_ref[group, :, at * piece : (at + 1) * piece] = chosen


def finish_kernel(
    sizes, at_ref, branch_ref, residual_ref, early_ref, summed_ref, other_ref, forward_ref, received_ref, ctx_ref
):
    ctx_ref[...] = (summed_ref[:, : ctx_ref.shape[1]] + other_ref[...].astype(F32)).astype(BF16)
    piece = sizes[-1]
    section, core = at_ref[0], at_ref[1]
    for group, at, first in by_group(*sizes):
        here = slice(first, first + piece)

        def term(of_section):
            mine, other = branch_ref[of_section, group, :, :piece], branch_ref[of_section, group, :, piece:]
            return jnp.where(core == at, mine, other).astype(F32)

        one, two = term(0), term(1)
        forward_ref[:, here] = (residual_ref[:, here].astype(F32) + jnp.where(section == 0, one, two)).astype(BF16)
        early = early_ref[:, here]
        received_ref[:, here] = jnp.where(section == 0, early, (early.astype(F32) + one).astype(BF16))


def local(kernel, at, arrays, shapes):
    whole = pl.BlockSpec(memory_space=pltpu.VMEM)
    return pl.pallas_call(
        kernel,
        out_shape=[jax.ShapeDtypeStruct(shape, BF16) for shape in shapes],
        in_specs=[pl.BlockSpec(memory_space=pltpu.SMEM)] + [whole] * len(arrays),
        out_specs=[whole] * len(shapes),
        compiler_params=pltpu.CompilerParams(vmem_limit_bytes=24 * 2**20),
    )(at, *arrays)


def shards(segment_input, context, out_proj, grad_output):
    residual = segment_input[0]
    contexts = context[0]
    weights = out_proj[0]
    upstream = grad_output[0]
    section, y, core, z, xh = (lax.axis_index(name) for name in ("section", "y", "core", "z", "xh"))
    n_y, n_core, n_z, n_xh = (lax.axis_size(name) for name in ("y", "core", "z", "xh"))
    own_count, model = upstream.shape
    group_tokens, width = contexts.shape
    piece = model // (n_y * n_core * n_xh)
    group = n_y * n_xh
    features = n_core * piece
    tokens = group_tokens * n_y
    z_tokens = own_count * n_xh
    block_tokens = own_count * group

    both = jnp.concatenate([contexts, swap(contexts, "xh")], 1)
    def rows(core_at, xh_at):
        return lax.dynamic_slice_in_dim(weights, ((y * n_core + core_at) * n_xh + xh_at) * piece, piece, 0)

    both, partner_rows = tie(both, rows(core, 1 - xh))
    came_rows = swap(partner_rows, "xh")
    other_rows = swap(came_rows, "core")
    block = jnp.concatenate(
        [jnp.concatenate([rows(core, xh), came_rows], 1), jnp.concatenate([rows(1 - core, xh), other_rows], 1)], 0
    )

    ctx_all = jnp.zeros((n_z, n_y, z_tokens, 2 * width), BF16)
    ctx_blocks, across = ring_gather(both, "y")
    ctx_blocks[n_y // 2] = jnp.concatenate(across, 0)
    for away, part in ctx_blocks.items():
        ctx_all = place(ctx_all, part.reshape(n_z, 1, z_tokens, 2 * width), (0, wrap(y + away, n_y), 0, 0))
    ctx_flat = ctx_all.reshape(tokens, 2 * width)

    sizes = (n_y, n_core, n_xh, piece)
    at = jnp.stack([section, core]).astype(jnp.int32)
    (spread,) = local(functools.partial(spread_kernel, sizes), at, [upstream], [(group, own_count, features)])
    spread = lax.all_to_all(spread, ("y", "xh"), 0, 0, tiled=True).reshape(block_tokens, features)
    grad_all = jnp.zeros((n_z, block_tokens, features), BF16)
    grad_blocks, far_blocks = ring_gather(spread, "z")
    for away, part in grad_blocks.items():
        grad_all = place(grad_all, part[None], (wrap(z + away, n_z), 0, 0))

    partial_branch = lax.dot_general(
        ctx_flat, block, (((1,), (1,)), ((), ())), preferred_element_type=F32
    ).astype(BF16).reshape(n_z, block_tokens, features)
    ring = ring_steps(lambda away: pick(partial_branch, wrap(z + away, n_z)), "z")
    *step, outgoing = tie(*next(ring), jnp.where(section == 0, residual, upstream))
    early = swap(outgoing, "section")
    step = ring.send(step)
    far = jnp.concatenate(far_blocks, 0)[None]
    grad_flat = place(grad_all, far, (wrap(z + n_z // 2, n_z), 0, 0)).reshape(tokens, features)
    partial_ctx = jnp.dot(grad_flat, block, preferred_element_type=F32).astype(BF16)
    *step, partial_ctx = tie(*step, partial_ctx)
    step = ring.send(step)
    norm_factor = 1.0 / math.sqrt(tokens * n_core)
    product = lax.dot_general(grad_flat, ctx_flat, (((0,), (0,)), ((), ())), preferred_element_type=F32)
    product, partial_ctx = tie((norm_factor * product).astype(BF16), partial_ctx)
    partial_ctx = partial_ctx.reshape(n_z, n_y, z_tokens, 2 * width)
    ctx_ring = ring_steps(lambda away: pick(partial_ctx, wrap(y + away, n_y), 1).reshape(group_tokens, 2 * width), "y")
    ctx_step = next(ctx_ring)
    other_product = swap(product[piece:], "core")
    *step, other_product, early = tie(*step, other_product, early)
    step = ring.send(step)
    ctx_step = ctx_ring.send(ctx_step)
    own_rows = add(product[:piece], other_product)
    half = piece // 2
    came_first = swap(own_rows[:half, width:], "xh")
    *ctx_step, came_first = tie(*ctx_step, came_first)
    came_last = swap(own_rows[half:, width:], "xh")
    branch = ring.send(step).astype(BF16)
    branch = branch.reshape(1, group, own_count, features)
    branch = jnp.concatenate([branch, branch], 0).reshape(2 * group, own_count, features)
    branch = lax.all_to_all(branch, ("section", "y", "xh"), 0, 0, tiled=True)

    summed = ctx_ring.send(ctx_step)
    other_ctx = swap(summed[:, width:].astype(BF16), "xh")
    branch, came_last = tie(branch, came_last)
    forward, received, ctx_grad = local(
        functools.partial(finish_kernel, sizes),
        at,
        [branch.reshape(2, group, own_count, features), residual, early, summed, other_ctx],
        [residual.shape, residual.shape, other_ctx.shape],
    )

    weight_grad = place(jnp.zeros((n_xh * piece, width), BF16), own_rows[:, :width], (xh * piece, 0))
    weight_grad = place(weight_grad, came_first, ((1 - xh) * piece, 0))
    weight_grad = place(weight_grad, came_last, ((1 - xh) * piece + half, 0))
    return (forward[None], received[None], ctx_grad[None], weight_grad[None])


def solution(mesh):
    fine = Mesh(mesh.devices.reshape(2, 4, 2, 8, 2), ("section", "y", "core", "z", "xh"))
    tokens = P("section", ("y", "core", "z", "xh"), None)
    heads = P("section", ("y", "core"), ("z", "xh"))
    return jax.shard_map(
        shards,
        mesh=fine,
        in_specs=(tokens, heads, P("section", None, ("z", "xh")), tokens),
        out_specs=(tokens, tokens, heads, heads),
        check_vma=False,
    )
```
